256 devices in a mesh: ctx: 32 (over z, y), seq: 8 (over x, core).
Axes of the slice: x: 4, y: 4, z: 8, core: 2. Of those that a mesh axis runs over, the one named last changes fastest.
Arguments:
- query_input: bfloat16 [8, 4096, 2048], P('seq', 'ctx'), may hold values from -6 to 6
- key_input: bfloat16 [8, 4096, 2048], P('seq', 'ctx'), may hold values from -6 to 6
- value_input: bfloat16 [8, 4096, 2048], P('seq', 'ctx'), may hold values from -6 to 6
- cotangent: bfloat16 [8, 4096, 2048], P('seq', 'ctx'), may hold values from -6 to 6
- residues: float32 [2048, 16], replicated, may hold values from -1.5 to 1.5
- decay_rates: float32 [2048, 16], replicated, as said below
Outputs:
- output: bfloat16 [8, 4096, 2048], P('seq', 'ctx')
- grad_query: bfloat16 [8, 4096, 2048], P('seq', 'ctx')
- grad_key: bfloat16 [8, 4096, 2048], P('seq', 'ctx')
- grad_value: bfloat16 [8, 4096, 2048], P('seq', 'ctx')
- grad_residues: float32 [2048, 16], replicated
The draws below stay inside these ranges and needn't reach their ends.
Inputs may be any that keep to these rules, and one draw needn't show every extreme that they name: `decay_rates`: every rate lies between 0.1 divided by 4096 and 1 divided by 30.
All inputs are finite; a program needn't handle non-finite values.
Results may differ from the reference program's by a relative error of at most 0.0013.
Values sent between devices are 32-bit elements; how exact they have to be, the bound alone decides.
No kernel may reach another device: no remote copies, remote signals or barrier semaphores. Data moves between devices by JAX's collectives and lax.ppermute only.
A program may use at most 192 MiB of HBM per device.

```python
import jax
import jax.numpy as jnp
from jax import lax

C = 2048
M = 16
TOK_DEV = 128
SEQ_LEN = 4096
BATCH = 8


def draw_decay_rates(key, part):
    key = jax.random.fold_in(key, 7)
    pick_key, slow_key, fast_key = jax.random.split(key, 3)
    share = 0.5
    slow = jax.random.uniform(pick_key, (C, M)) < share
    slow_rate = jnp.exp(jax.random.uniform(slow_key, (C, M), minval=jnp.log(0.05), maxval=0.0)) * (2.0 / SEQ_LEN)
    fast_rate = jnp.exp(jax.random.uniform(fast_key, (C, M), minval=jnp.log(1.0 / (4 * TOK_DEV)), maxval=jnp.log(1.0 / 30)))
    return jnp.where(slow, slow_rate, fast_rate).astype(jnp.float32)


def levels(own_key, dims, shards, least, high):
    loudness, own = 1.0, jax.random.fold_in(own_key, 6)
    for dim, shards_of in shards:
        heights = jnp.exp(jax.random.uniform(jax.random.fold_in(own, dim), (shards_of,), jnp.float32, least / len(shards), high / len(shards)))
        loudness = loudness * jnp.repeat(heights, dims[dim] // shards_of).reshape([-1 if axis == dim else 1 for axis in range(len(dims))])
    return loudness


def gaussian(stream_key, dims, scale, most, cuts=(), dtype=jnp.bfloat16):
    result = scale * jax.random.normal(stream_key, dims, jnp.float32)
    if cuts:
        result = result * levels(stream_key, dims, cuts, -0.22, 0.18)
    return jnp.clip(result, -most, most).astype(dtype)


def setup_inputs(seed: int = 0) -> dict:
    arg_keys = jax.random.split(jax.random.key(seed), 7)
    query_input = gaussian(arg_keys[0], (BATCH, SEQ_LEN, C), 1.0, 6.0, ((0, 8), (1, 32)))
    key_input = gaussian(arg_keys[1], (BATCH, SEQ_LEN, C), 1.0, 6.0, ((0, 8), (1, 32)))
    value_input = gaussian(arg_keys[2], (BATCH, SEQ_LEN, C), 1.0, 6.0, ((0, 8), (1, 32)))
    cotangent = gaussian(arg_keys[3], (BATCH, SEQ_LEN, C), 1.0, 6.0, ((0, 8), (1, 32)))
    residues = gaussian(arg_keys[4], (C, M), 0.25, 1.5, (), jnp.float32)
    decay_rates = draw_decay_rates(jax.random.fold_in(arg_keys[6], 71), 0)
    return dict(query_input=query_input, key_input=key_input, value_input=value_input, cotangent=cotangent, residues=residues, decay_rates=decay_rates)


def filter_taps(residues, decay_rates, scaling, steps):
    taps = jnp.zeros((SEQ_LEN, C), jnp.float32)
    for mode_index in range(M):
        weight = residues[:, mode_index] * scaling[:, mode_index]
        taps = taps + weight[None, :] * jnp.exp(-steps[:, None] * decay_rates[None, :, mode_index])
    return taps

def reference(query_input, key_input, value_input, cotangent, residues, decay_rates):
    scaling = jnp.sqrt(-jnp.expm1(-2.0 * decay_rates))
    steps = jnp.arange(SEQ_LEN).astype(jnp.float32)
    taps = filter_taps(residues, decay_rates, scaling, steps)
    padded = 2 * SEQ_LEN
    tap_spec = jnp.fft.rfft(taps, n=padded, axis=0)

    def per_sequence(carried, sequence_parts):
        query_rows, key_rows, value_rows, cot_rows = sequence_parts
        query_wide = query_rows.astype(jnp.float32)
        key_wide = key_rows.astype(jnp.float32)
        value_wide = value_rows.astype(jnp.float32)
        cot_wide = cot_rows.astype(jnp.float32)
        mixed = key_wide * value_wide
        adjoint = cot_wide * query_wide
        mix_spec = jnp.fft.rfft(mixed, n=padded, axis=0)
        adj_spec = jnp.fft.rfft(adjoint, n=padded, axis=0)
        convolved = jnp.fft.irfft(mix_spec * tap_spec, n=padded, axis=0)[:SEQ_LEN]
        grad_mixed = jnp.fft.irfft(adj_spec * jnp.conj(tap_spec), n=padded, axis=0)[:SEQ_LEN]
        lagged = jnp.fft.irfft(adj_spec * jnp.conj(mix_spec), n=padded, axis=0)[:SEQ_LEN]
        results = ((query_wide * convolved).astype(jnp.bfloat16), (cot_wide * convolved).astype(jnp.bfloat16), (grad_mixed * value_wide).astype(jnp.bfloat16), (grad_mixed * key_wide).astype(jnp.bfloat16))
        return (carried + lagged, results)
    lagged, stacked = lax.scan(per_sequence, jnp.zeros((SEQ_LEN, C), jnp.float32), (query_input, key_input, value_input, cotangent))
    output, grad_query, grad_key, grad_value = stacked
    columns = []
    for mode_index in range(M):
        decay = jnp.exp(-steps[:, None] * decay_rates[None, :, mode_index])
        columns.append(lax.optimization_barrier(jnp.sum(lagged * decay, axis=0)))
    grad_residues = jnp.stack(columns, axis=1) * scaling / (BATCH * SEQ_LEN)
    return (output, grad_query, grad_key, grad_value, grad_residues)
```

```python
import functools

import jax
import jax.numpy as jnp
from jax import lax
from jax.experimental import pallas as pl
from jax.experimental.pallas import tpu as pltpu
from jax.sharding import PartitionSpec as P

LANES = 128
SUBS = 8
MODES_TILE = 8
F32 = jnp.float32


def sub_index():
    return lax.broadcasted_iota(jnp.int32, (SUBS, LANES), 0)


def prefix_over_subs(state, decays, sub):
    total = state
    for step, decay in zip((1, 2, 4), decays, strict=True):
        total = total + jnp.where(sub >= step, pltpu.roll(total, step, 0), 0.0) * decay
    return total


def suffix_over_subs(state, decays, sub):
    total = state
    for step, decay in zip((1, 2, 4), decays, strict=True):
        total = total + jnp.where(sub < SUBS - step, pltpu.roll(total, SUBS - step, 0), 0.0) * decay
    return total


def rows_of(tile):
    return [jnp.broadcast_to(tile[m : m + 1], (SUBS, LANES)) for m in range(MODES_TILE)]


def states_kernel(
    query_ref, key_ref, value_ref, cot_ref, rates_ref, packed_ref, before_ref, after_ref, u_ref, a_ref
):
    tokens, width = query_ref.shape
    steps = tokens // SUBS
    modes = rates_ref.shape[0]
    sub = sub_index()

    def block(index, carry):
        lanes = pl.ds(pl.multiple_of(index * LANES, LANES), LANES)
        u_ref[...] = key_ref[:, lanes].astype(F32) * value_ref[:, lanes].astype(F32)
        a_ref[...] = cot_ref[:, lanes].astype(F32) * query_ref[:, lanes].astype(F32)
        for half in range(modes // MODES_TILE):
            rates = rates_ref[half * MODES_TILE : (half + 1) * MODES_TILE, lanes]
            lam = rows_of(jnp.exp(-rates))
            zero = jnp.zeros((SUBS, LANES), F32)
            fwd = [zero] * MODES_TILE
            grad = [zero] * MODES_TILE
            bwd = [zero] * MODES_TILE
            for i in range(steps):
                u = u_ref[pl.ds(i, SUBS, stride=steps), :]
                a = a_ref[pl.ds(i, SUBS, stride=steps), :]
                back = a_ref[pl.ds(steps - 1 - i, SUBS, stride=steps), :]
                for m in range(MODES_TILE):
                    fwd[m] = lam[m] * fwd[m] + u
                    grad[m] = grad[m] + a * fwd[m]
                    bwd[m] = lam[m] * bwd[m] + back
            decays = [rows_of(jnp.exp(rates * -float(steps * k))) for k in (1, 2, 4)]
            for m in range(MODES_TILE):
                decay = [d[m] for d in decays]
                upto = prefix_over_subs(fwd[m], decay, sub)
                down = suffix_over_subs(bwd[m], decay, sub)
                before = jnp.where(sub >= 1, pltpu.roll(upto, 1, 0), 0.0)
                after = jnp.where(sub < SUBS - 1, pltpu.roll(down, SUBS - 1, 0), 0.0)
                inner = grad[m] + lam[m] * bwd[m] * before
                before_ref[index, half * MODES_TILE + m] = before
                after_ref[index, half * MODES_TILE + m] = after
                packed_ref[half, index, m : m + 1, :] = upto[SUBS - 1 : SUBS]
                packed_ref[half, index, MODES_TILE + m : MODES_TILE + m + 1, :] = down[0:1]
                packed_ref[half, index, 2 * MODES_TILE + m : 2 * MODES_TILE + m + 1, :] = jnp.sum(
                    inner, axis=0, keepdims=True
                )
        return carry

    lax.fori_loop(0, width // LANES, block, 0)


def local_kernel(
    query_ref,
    key_ref,
    value_ref,
    cot_ref,
    rates_ref,
    weight_ref,
    before_ref,
    after_ref,
    conv_ref,
    grad_ref,
    u_ref,
    a_ref,
    y_ref,
    g_ref,
):
    tokens, width = query_ref.shape
    steps = tokens // SUBS
    modes = rates_ref.shape[0]

    def block(index, carry):
        lanes = pl.ds(pl.multiple_of(index * LANES, LANES), LANES)
        u_ref[...] = key_ref[:, lanes].astype(F32) * value_ref[:, lanes].astype(F32)
        a_ref[...] = cot_ref[:, lanes].astype(F32) * query_ref[:, lanes].astype(F32)
        for half in range(modes // MODES_TILE):
            picked = slice(half * MODES_TILE, (half + 1) * MODES_TILE)
            lam = rows_of(jnp.exp(-rates_ref[picked, lanes]))
            weight = rows_of(weight_ref[picked, lanes])
            fwd = [before_ref[index, half * MODES_TILE + m] for m in range(MODES_TILE)]
            for i in range(steps):
                rows = pl.ds(i, SUBS, stride=steps)
                u = u_ref[rows, :]
                total = y_ref[rows, :] if half else None
                for m in range(MODES_TILE):
                    fwd[m] = lam[m] * fwd[m] + u
                    term = weight[m] * fwd[m]
                    total = term if total is None else total + term
                y_ref[rows, :] = total
            bwd = [after_ref[index, half * MODES_TILE + m] for m in range(MODES_TILE)]
            for i in reversed(range(steps)):
                rows = pl.ds(i, SUBS, stride=steps)
                a = a_ref[rows, :]
                total = g_ref[rows, :] if half else None
                for m in range(MODES_TILE):
                    bwd[m] = lam[m] * bwd[m] + a
                    term = weight[m] * bwd[m]
                    total = term if total is None else total + term
                g_ref[rows, :] = total
        conv_ref[:, lanes] = y_ref[...]
        grad_ref[:, lanes] = g_ref[...]
        return carry

    lax.fori_loop(0, width // LANES, block, 0)


def scan_kernel(chunk_tokens, per_half, share, states_ref, rates_ref, weight_ref, scaling_ref, out_ref, part_ref):
    chunks = states_ref.shape[0]
    rank = lax.axis_index("ctx")
    rows = pl.ds(pl.multiple_of((rank // per_half) * MODES_TILE, MODES_TILE), MODES_TILE)
    lanes = pl.ds(pl.multiple_of((rank % per_half) * LANES, LANES), LANES)
    rates = rates_ref[rows, lanes]
    lam = jnp.exp(-rates)
    jump = jnp.exp(rates * -float(chunk_tokens))
    entry = weight_ref[rows, lanes] * lam
    zero = jnp.zeros((MODES_TILE, LANES), F32)
    fwd, cross, inner = zero, zero, zero
    for j in range(chunks):
        out_ref[j, 0:MODES_TILE] = entry * fwd
        cross = cross + states_ref[j, MODES_TILE : 2 * MODES_TILE] * fwd
        inner = inner + states_ref[j, 2 * MODES_TILE : 3 * MODES_TILE]
        fwd = jump * fwd + states_ref[j, 0:MODES_TILE]
    bwd = zero
    for j in reversed(range(chunks)):
        out_ref[j, MODES_TILE : 2 * MODES_TILE] = entry * bwd
        bwd = jump * bwd + states_ref[j, MODES_TILE : 2 * MODES_TILE]
    part = (inner + lam * cross) * scaling_ref[rows, lanes] * share
    for s in range(part_ref.shape[0]):
        part_ref[s] = part


def pack_kernel(states_ref, parts_ref, out_ref):
    total = parts_ref[0]
    for s in range(1, parts_ref.shape[0]):
        total = total + parts_ref[s]
    for j in range(states_ref.shape[0]):
        out_ref[j, 0 : 2 * MODES_TILE] = states_ref[j]
        out_ref[j, 2 * MODES_TILE : 3 * MODES_TILE] = total


def output_kernel(
    query_ref,
    key_ref,
    value_ref,
    cot_ref,
    rates_ref,
    conv_ref,
    grad_ref,
    entry_ref,
    out_ref,
    grad_query_ref,
    grad_key_ref,
    grad_value_ref,
    grad_res_ref,
    y_ref,
    g_ref,
):
    tokens, width = query_ref.shape
    modes = rates_ref.shape[0]
    groups = tokens // SUBS
    sub = sub_index().astype(F32)

    def block(index, carry):
        lanes = pl.ds(pl.multiple_of(index * LANES, LANES), LANES)
        for half in range(modes // MODES_TILE):
            picked = slice(half * MODES_TILE, (half + 1) * MODES_TILE)
            rates = rates_ref[picked, lanes]
            row = rows_of(rates)
            jump = rows_of(jnp.exp(rates * -float(SUBS)))
            early = rows_of(entry_ref[half, index, 0:MODES_TILE, :])
            late = rows_of(entry_ref[half, index, MODES_TILE : 2 * MODES_TILE, :])
            grad_res_ref[picked, lanes] = entry_ref[half, index, 2 * MODES_TILE : 3 * MODES_TILE, :]
            fwd = [early[m] * jnp.exp(-row[m] * sub) for m in range(MODES_TILE)]
            bwd = [late[m] * jnp.exp(-row[m] * (SUBS - 1 - sub)) for m in range(MODES_TILE)]
            for i in range(groups):
                rows = slice(i * SUBS, (i + 1) * SUBS)
                total = y_ref[rows, :] if half else conv_ref[rows, lanes]
                for m in range(MODES_TILE):
                    total = total + fwd[m]
                    fwd[m] = fwd[m] * jump[m]
                y_ref[rows, :] = total
                rows = slice((groups - 1 - i) * SUBS, (groups - i) * SUBS)
                total = g_ref[rows, :] if half else grad_ref[rows, lanes]
                for m in range(MODES_TILE):
                    total = total + bwd[m]
                    bwd[m] = bwd[m] * jump[m]
                g_ref[rows, :] = total
        y = y_ref[...]
        g = g_ref[...]
        out_ref[:, lanes] = (query_ref[:, lanes].astype(F32) * y).astype(out_ref.dtype)
        grad_query_ref[:, lanes] = (cot_ref[:, lanes].astype(F32) * y).astype(out_ref.dtype)
        grad_key_ref[:, lanes] = (value_ref[:, lanes].astype(F32) * g).astype(out_ref.dtype)
        grad_value_ref[:, lanes] = (key_ref[:, lanes].astype(F32) * g).astype(out_ref.dtype)
        return carry

    lax.fori_loop(0, width // LANES, block, 0)


def on_device(query_input, key_input, value_input, cotangent, residues, decay_rates):
    tokens, channels = query_input.shape[1:]
    modes = residues.shape[1]
    ctx_count = lax.axis_size("ctx")
    seq_count = lax.axis_size("seq")
    blocks = channels // LANES
    halves = modes // MODES_TILE
    per_step = 4
    width = per_step * LANES
    grid = (blocks // per_step,)
    signals = [s[0] for s in (query_input, key_input, value_input, cotangent)]
    rates = decay_rates.T

    signal_spec = pl.BlockSpec((tokens, width), lambda i: (0, i))
    mode_spec = pl.BlockSpec((modes, width), lambda i: (0, i))
    packed_spec = pl.BlockSpec((halves, per_step, 3 * MODES_TILE, LANES), lambda i: (0, i, 0, 0))
    border_spec = pl.BlockSpec((per_step, modes, SUBS, LANES), lambda i: (i, 0, 0, 0))
    border_shape = jax.ShapeDtypeStruct((blocks, modes, SUBS, LANES), F32)
    whole = jax.ShapeDtypeStruct((tokens, channels), F32)
    square = pltpu.VMEM((tokens, LANES), F32)

    def cost(ops, moved):
        return pl.CostEstimate(
            flops=ops * tokens * channels, bytes_accessed=moved * tokens * channels, transcendentals=0
        )

    packed, before, after = pl.pallas_call(
        states_kernel,
        grid=grid,
        in_specs=[signal_spec] * 4 + [mode_spec],
        out_specs=[packed_spec, border_spec, border_spec],
        out_shape=[
            jax.ShapeDtypeStruct((halves, blocks, 3 * MODES_TILE, LANES), F32),
            border_shape,
            border_shape,
        ],
        scratch_shapes=[square] * 2,
        cost_estimate=cost(96, 16),
        name="states",
    )(*signals, rates)

    late_rates, late_residues, packed = lax.optimization_barrier((rates, residues.T, packed))
    scaling = jnp.sqrt(-jnp.expm1(-2.0 * late_rates))
    weight = late_residues * scaling

    gathered = lax.all_to_all(
        packed.reshape(ctx_count, 3 * MODES_TILE, LANES), "ctx", split_axis=0, concat_axis=0, tiled=True
    )

    conv, grad = pl.pallas_call(
        local_kernel,
        grid=grid,
        in_specs=[signal_spec] * 4 + [mode_spec] * 2 + [border_spec] * 2,
        out_specs=[signal_spec] * 2,
        out_shape=[whole] * 2,
        scratch_shapes=[square] * 4,
        cost_estimate=cost(128, 24),
        name="local",
    )(*signals, rates, weight, before, after)

    borders, part = pl.pallas_call(
        functools.partial(scan_kernel, tokens, blocks, 1.0 / (tokens * ctx_count * seq_count)),
        out_shape=[
            jax.ShapeDtypeStruct((ctx_count, 2 * MODES_TILE, LANES), F32),
            jax.ShapeDtypeStruct((seq_count, MODES_TILE, LANES), F32),
        ],
        name="scan",
    )(gathered, rates, weight, scaling)

    parts = lax.all_to_all(part, "seq", split_axis=0, concat_axis=0, tiled=True)
    repacked = pl.pallas_call(
        pack_kernel,
        out_shape=jax.ShapeDtypeStruct((ctx_count, 3 * MODES_TILE, LANES), F32),
        name="pack",
    )(borders, parts)
    returned = lax.all_to_all(repacked, "ctx", split_axis=0, concat_axis=0, tiled=True)

    half_type = query_input.dtype
    result = jax.ShapeDtypeStruct((tokens, channels), half_type)
    output, grad_query, grad_key, grad_value, grad_residues = pl.pallas_call(
        output_kernel,
        grid=grid,
        in_specs=[signal_spec] * 4 + [mode_spec] + [signal_spec] * 2 + [packed_spec],
        out_specs=[signal_spec] * 4 + [mode_spec],
        out_shape=[result] * 4 + [jax.ShapeDtypeStruct((modes, channels), F32)],
        scratch_shapes=[square] * 2,
        cost_estimate=cost(64, 24),
        name="outputs",
    )(*signals, rates, conv, grad, returned.reshape(halves, blocks, 3 * MODES_TILE, LANES))
    return (output[None], grad_query[None], grad_key[None], grad_value[None], grad_residues.T)


def solution(mesh):
    split = P("seq", "ctx", None)
    return jax.shard_map(
        on_device,
        mesh=mesh,
        in_specs=(split, split, split, split, P(), P()),
        out_specs=(split, split, split, split, P()),
        check_vma=False,
    )
```

```python
import functools

import jax
import jax.numpy as jnp
from jax import lax
from jax.experimental import pallas as pl
from jax.experimental.pallas import tpu as pltpu
from jax.sharding import PartitionSpec as P

LANES = 128
SUBS = 8
MODES_TILE = 8
F32 = jnp.float32
GROUPS = 4
PITCH = 17
SMALL_VMEM = 12 * 1024 * 1024
STATES_VMEM = 58 * 1024 * 1024
OUTPUTS_VMEM = 51 * 1024 * 1024


def sub_index():
    return lax.broadcasted_iota(jnp.int32, (SUBS, LANES), 0)


def rows_of(tile):
    return [jnp.broadcast_to(tile[m : m + 1], (SUBS, LANES)) for m in range(MODES_TILE)]


def states_kernel(
    query_hbm,
    key_hbm,
    value_hbm,
    cot_hbm,
    rates_hbm,
    packed_hbm,
    before_hbm,
    after_hbm,
    query_ref,
    key_ref,
    value_ref,
    cot_ref,
    rates_ref,
    packed_ref,
    before_ref,
    after_ref,
    rates_arrived,
    arrived,
    sent,
    u_ref,
    a_ref,
    lag_ref,
    lag_sum_ref,
    fwd_ref,
    bwd_ref,
):
    tokens, width = query_ref.shape
    steps = tokens // SUBS
    modes = rates_ref.shape[0]
    groups = arrived.shape[1]
    span = width // groups
    pairs = ((query_hbm, query_ref), (key_hbm, key_ref), (value_hbm, value_ref), (cot_hbm, cot_ref))

    def fetches(group):
        lanes = pl.ds(pl.multiple_of(group * span, span), span)
        return [
            pltpu.make_async_copy(source.at[:, lanes], target.at[:, lanes], arrived.at[n, group])
            for n, (source, target) in enumerate(pairs)
        ]

    def stores(group):
        count = span // LANES
        part = pl.ds(group * count, count)
        return [
            pltpu.make_async_copy(packed_ref.at[:, part], packed_hbm.at[:, part], sent.at[0, group]),
            pltpu.make_async_copy(before_ref.at[part], before_hbm.at[part], sent.at[1, group]),
            pltpu.make_async_copy(after_ref.at[part], after_hbm.at[part], sent.at[2, group]),
        ]

    rates_fetch = pltpu.make_async_copy(rates_hbm, rates_ref, rates_arrived)
    for group in range(groups):
        for fetch in fetches(group):
            fetch.start()
        if group == 0:
            rates_fetch.start()
    rates_fetch.wait()

    def block(index, carry):
        lanes = pl.ds(pl.multiple_of(index * LANES, LANES), LANES)
        mixed = key_ref[:, lanes].astype(F32) * value_ref[:, lanes].astype(F32)
        adjoint = cot_ref[:, lanes].astype(F32) * query_ref[:, lanes].astype(F32)
        for s in range(SUBS):
            u_ref[s * PITCH : s * PITCH + steps, :] = mixed[s * steps : (s + 1) * steps]
            a_ref[s * PITCH : s * PITCH + steps, :] = adjoint[s * steps : (s + 1) * steps]
        u = [u_ref[pl.ds(i, SUBS, stride=PITCH), :] for i in range(steps)]
        a = [a_ref[pl.ds(i, SUBS, stride=PITCH), :] for i in range(steps)]
        for lag in range(steps):
            total = a[lag] * u[0]
            for i in range(1, steps - lag):
                total = total + a[lag + i] * u[i]
            lag_ref[lag * SUBS : (lag + 1) * SUBS, :] = total
        for group in range(steps // SUBS):
            total = None
            for s in range(SUBS):
                term = lag_ref[pl.ds(group * SUBS * SUBS + s, SUBS, stride=SUBS), :]
                total = term if total is None else total + term
            lag_sum_ref[group * SUBS : (group + 1) * SUBS, :] = total
        for half in range(modes // MODES_TILE):
            rates = rates_ref[half * MODES_TILE : (half + 1) * MODES_TILE, lanes]
            lam_tile = jnp.exp(-rates)
            lam = rows_of(lam_tile)
            fwd = [u_ref[pl.ds(0, SUBS, stride=PITCH), :]] * MODES_TILE
            bwd = [a_ref[pl.ds(steps - 1, SUBS, stride=PITCH), :]] * MODES_TILE
            for i in range(1, steps):
                front = u_ref[pl.ds(i, SUBS, stride=PITCH), :]
                back = a_ref[pl.ds(steps - 1 - i, SUBS, stride=PITCH), :]
                for m in range(MODES_TILE):
                    fwd[m] = lam[m] * fwd[m] + front
                    bwd[m] = lam[m] * bwd[m] + back
            for m in range(MODES_TILE):
                fwd_ref[m * SUBS : (m + 1) * SUBS, :] = fwd[m]
                bwd_ref[m * SUBS : (m + 1) * SUBS, :] = bwd[m]
            jump = jnp.exp(rates * -float(steps))
            zero = jnp.zeros((MODES_TILE, LANES), F32)
            before, after, cross, inner = zero, zero, zero, zero
            for s in range(SUBS):
                rows = pl.ds(s, MODES_TILE, stride=SUBS)
                before_ref[index, half, rows, :] = before
                cross = cross + bwd_ref[rows, :] * before
                before = jump * before + fwd_ref[rows, :]
            for s in reversed(range(SUBS)):
                rows = pl.ds(s, MODES_TILE, stride=SUBS)
                after_ref[index, half, rows, :] = after
                after = jump * after + bwd_ref[rows, :]
            for lag in reversed(range(steps)):
                inner = inner * lam_tile + lag_sum_ref[lag : lag + 1, :]
            packed_ref[half, index, 0:MODES_TILE, :] = before
            packed_ref[half, index, MODES_TILE : 2 * MODES_TILE, :] = after
            packed_ref[half, index, 2 * MODES_TILE : 3 * MODES_TILE, :] = inner + lam_tile * cross
        return carry

    def column(group, carry):
        for fetch in fetches(group):
            fetch.wait()
        per_group = span // LANES
        carry = lax.fori_loop(group * per_group, (group + 1) * per_group, block, carry)
        for store in stores(group):
            store.start()
        return carry

    lax.fori_loop(0, groups, column, 0)
    for group in range(groups):
        for store in stores(group):
            store.wait()


def local_kernel(
    query_ref,
    key_ref,
    value_ref,
    cot_ref,
    rates_ref,
    weight_ref,
    before_ref,
    after_ref,
    conv_ref,
    grad_ref,
    u_ref,
    a_ref,
    y_ref,
    g_ref,
):
    tokens, width = query_ref.shape
    steps = tokens // SUBS
    modes = rates_ref.shape[0]

    def block(index, carry):
        lanes = pl.ds(pl.multiple_of(index * LANES, LANES), LANES)
        u_ref[...] = key_ref[:, lanes].astype(F32) * value_ref[:, lanes].astype(F32)
        a_ref[...] = cot_ref[:, lanes].astype(F32) * query_ref[:, lanes].astype(F32)
        for half in range(modes // MODES_TILE):
            picked = slice(half * MODES_TILE, (half + 1) * MODES_TILE)
            lam = rows_of(jnp.exp(-rates_ref[picked, lanes]))
            weight = rows_of(weight_ref[picked, lanes])
            fwd = [before_ref[index, half, m * SUBS : (m + 1) * SUBS, :] for m in range(MODES_TILE)]
            for i in range(steps):
                rows = pl.ds(i, SUBS, stride=steps)
                u = u_ref[rows, :]
                total = y_ref[rows, :] if half else None
                for m in range(MODES_TILE):
                    fwd[m] = lam[m] * fwd[m] + u
                    term = weight[m] * fwd[m]
                    total = term if total is None else total + term
                y_ref[rows, :] = total
            bwd = [after_ref[index, half, m * SUBS : (m + 1) * SUBS, :] for m in range(MODES_TILE)]
            for i in reversed(range(steps)):
                rows = pl.ds(i, SUBS, stride=steps)
                a = a_ref[rows, :]
                total = g_ref[rows, :] if half else None
                for m in range(MODES_TILE):
                    bwd[m] = lam[m] * bwd[m] + a
                    term = weight[m] * bwd[m]
                    total = term if total is None else total + term
                g_ref[rows, :] = total
        conv_ref[:, lanes] = y_ref[...]
        grad_ref[:, lanes] = g_ref[...]
        return carry

    lax.fori_loop(0, width // LANES, block, 0)


def scan_kernel(chunk_tokens, per_half, share, states_ref, rates_ref, weight_ref, scaling_ref, out_ref, part_ref):
    chunks = states_ref.shape[0]
    rank = lax.axis_index("ctx")
    rows = pl.ds(pl.multiple_of((rank // per_half) * MODES_TILE, MODES_TILE), MODES_TILE)
    lanes = pl.ds(pl.multiple_of((rank % per_half) * LANES, LANES), LANES)
    rates = rates_ref[rows, lanes]
    lam = jnp.exp(-rates)
    jump = jnp.exp(rates * -float(chunk_tokens))
    entry = weight_ref[rows, lanes] * lam
    zero = jnp.zeros((MODES_TILE, LANES), F32)
    fwd, cross, inner = zero, zero, zero
    for j in range(chunks):
        out_ref[j, 0:MODES_TILE] = entry * fwd
        cross = cross + states_ref[j, MODES_TILE : 2 * MODES_TILE] * fwd
        inner = inner + states_ref[j, 2 * MODES_TILE : 3 * MODES_TILE]
        fwd = jump * fwd + states_ref[j, 0:MODES_TILE]
    bwd = zero
    for j in reversed(range(chunks)):
        out_ref[j, MODES_TILE : 2 * MODES_TILE] = entry * bwd
        bwd = jump * bwd + states_ref[j, MODES_TILE : 2 * MODES_TILE]
    part = (inner + lam * cross) * scaling_ref[rows, lanes] * share
    for s in range(part_ref.shape[0]):
        part_ref[s] = part


def pack_kernel(states_ref, parts_ref, out_ref):
    total = parts_ref[0]
    for s in range(1, parts_ref.shape[0]):
        total = total + parts_ref[s]
    for j in range(out_ref.shape[0]):
        out_ref[j, 0 : 2 * MODES_TILE] = states_ref[j]
        out_ref[j, 2 * MODES_TILE : 3 * MODES_TILE] = total


def output_kernel(
    query_ref,
    key_ref,
    value_ref,
    cot_ref,
    rates_ref,
    conv_hbm,
    grad_hbm,
    entry_ref,
    out_hbm,
    grad_query_hbm,
    grad_key_hbm,
    grad_value_hbm,
    grad_res_hbm,
    grad_res_ref,
    conv_ref,
    grad_ref,
    out_ref,
    grad_query_ref,
    grad_key_ref,
    grad_value_ref,
    arrived,
    sent,
    y_ref,
    g_ref,
):
    tokens, width = query_ref.shape
    modes = rates_ref.shape[0]
    groups = tokens // SUBS
    sub = sub_index().astype(F32)
    columns = sent.shape[1]
    span = width // columns
    pairs = (
        (out_ref, out_hbm),
        (grad_query_ref, grad_query_hbm),
        (grad_key_ref, grad_key_hbm),
        (grad_value_ref, grad_value_hbm),
        (grad_res_ref, grad_res_hbm),
    )

    inputs = (
        (conv_hbm, conv_ref),
        (grad_hbm, grad_ref),
    )

    def fetches(column):
        lanes = pl.ds(pl.multiple_of(column * span, span), span)
        return [
            pltpu.make_async_copy(source.at[:, lanes], target.at[:, lanes], arrived.at[n, column])
            for n, (source, target) in enumerate(inputs)
        ]

    for column in range(columns):
        for fetch in fetches(column):
            fetch.start()

    def stores(column):
        lanes = pl.ds(pl.multiple_of(column * span, span), span)
        return [
            pltpu.make_async_copy(source.at[:, lanes], target.at[:, lanes], sent.at[n, column])
            for n, (source, target) in enumerate(pairs)
        ]

    def entry(index, carry):
        lanes = pl.ds(pl.multiple_of(index * LANES, LANES), LANES)
        for half in range(modes // MODES_TILE):
            picked = slice(half * MODES_TILE, (half + 1) * MODES_TILE)
            rates = rates_ref[picked, lanes]
            row = rows_of(rates)
            jump = rows_of(jnp.exp(rates * -float(SUBS)))
            early = rows_of(entry_ref[half, index, 0:MODES_TILE, :])
            late = rows_of(entry_ref[half, index, MODES_TILE : 2 * MODES_TILE, :])
            grad_res_ref[picked, lanes] = entry_ref[half, index, 2 * MODES_TILE : 3 * MODES_TILE, :]
            fwd = [early[m] * jnp.exp(-row[m] * sub) for m in range(MODES_TILE)]
            bwd = [late[m] * jnp.exp(-row[m] * (SUBS - 1 - sub)) for m in range(MODES_TILE)]
            for i in range(groups):
                rows = slice(i * SUBS, (i + 1) * SUBS)
                total = y_ref[rows, lanes] if half else None
                for m in range(MODES_TILE):
                    total = fwd[m] if total is None else total + fwd[m]
                    fwd[m] = fwd[m] * jump[m]
                y_ref[rows, lanes] = total
                rows = slice((groups - 1 - i) * SUBS, (groups - i) * SUBS)
                total = g_ref[rows, lanes] if half else None
                for m in range(MODES_TILE):
                    total = bwd[m] if total is None else total + bwd[m]
                    bwd[m] = bwd[m] * jump[m]
                g_ref[rows, lanes] = total
        return carry

    def finish(index, carry):
        lanes = pl.ds(pl.multiple_of(index * LANES, LANES), LANES)
        y = y_ref[:, lanes] + conv_ref[:, lanes]
        g = g_ref[:, lanes] + grad_ref[:, lanes]
        out_ref[:, lanes] = (query_ref[:, lanes].astype(F32) * y).astype(out_ref.dtype)
        grad_query_ref[:, lanes] = (cot_ref[:, lanes].astype(F32) * y).astype(out_ref.dtype)
        grad_key_ref[:, lanes] = (value_ref[:, lanes].astype(F32) * g).astype(out_ref.dtype)
        grad_value_ref[:, lanes] = (key_ref[:, lanes].astype(F32) * g).astype(out_ref.dtype)
        return carry

    def column_step(column, carry):
        first, last = column * (span // LANES), (column + 1) * (span // LANES)
        carry = lax.fori_loop(first, last, entry, carry)
        for fetch in fetches(column):
            fetch.wait()
        carry = lax.fori_loop(first, last, finish, carry)
        for store in stores(column):
            store.start()
        return carry

    lax.fori_loop(0, columns, column_step, 0)
    for column in range(columns):
        for store in stores(column):
            store.wait()


def on_device(query_input, key_input, value_input, cotangent, residues, decay_rates):
    tokens, channels = query_input.shape[1:]
    modes = residues.shape[1]
    ctx_count = lax.axis_size("ctx")
    seq_count = lax.axis_size("seq")
    blocks = channels // LANES
    halves = modes // MODES_TILE
    signals = [s[0] for s in (query_input, key_input, value_input, cotangent)]
    rates = decay_rates.T

    here = pl.BlockSpec(memory_space=pltpu.VMEM)
    there = pl.BlockSpec(memory_space=pltpu.HBM)
    border = jax.ShapeDtypeStruct((blocks, halves, MODES_TILE * SUBS, LANES), F32)
    whole = jax.ShapeDtypeStruct((tokens, channels), F32)
    square = pltpu.VMEM((tokens, LANES), F32)
    tile = pltpu.VMEM((MODES_TILE * SUBS, LANES), F32)
    signal_type = query_input.dtype
    signal_buffer = pltpu.VMEM((tokens, channels), signal_type)
    small = pltpu.CompilerParams(vmem_limit_bytes=SMALL_VMEM)

    def cost(ops, moved):
        return pl.CostEstimate(
            flops=ops * tokens * channels, bytes_accessed=moved * tokens * channels, transcendentals=0
        )

    packed, before, after = pl.pallas_call(
        states_kernel,
        in_specs=[there] * 5,
        out_specs=[there] * 3,
        out_shape=[jax.ShapeDtypeStruct((halves, blocks, 3 * MODES_TILE, LANES), F32), border, border],
        scratch_shapes=[signal_buffer] * 4
        + [
            pltpu.VMEM((modes, channels), F32),
            pltpu.VMEM((halves, blocks, 3 * MODES_TILE, LANES), F32),
            pltpu.VMEM(border.shape, F32),
            pltpu.VMEM(border.shape, F32),
            pltpu.SemaphoreType.DMA(()),
            pltpu.SemaphoreType.DMA((4, GROUPS)),
            pltpu.SemaphoreType.DMA((3, GROUPS)),
            pltpu.VMEM((SUBS * PITCH, LANES), F32),
            pltpu.VMEM((SUBS * PITCH, LANES), F32),
            square,
            pltpu.VMEM((tokens // SUBS, LANES), F32),
            tile,
            tile,
        ],
        compiler_params=pltpu.CompilerParams(vmem_limit_bytes=STATES_VMEM),
        cost_estimate=cost(96, 16),
        name="states",
    )(*signals, rates)

    late_rates, late_residues, packed = lax.optimization_barrier((rates, residues.T, packed))
    scaling = jnp.sqrt(-jnp.expm1(-2.0 * late_rates))
    weight = late_residues * scaling

    gathered = lax.all_to_all(
        packed.reshape(ctx_count, 3 * MODES_TILE, LANES), "ctx", split_axis=0, concat_axis=0, tiled=True
    )

    per_step = blocks // GROUPS
    signal_spec = pl.BlockSpec((tokens, per_step * LANES), lambda i: (0, i))
    mode_spec = pl.BlockSpec((modes, per_step * LANES), lambda i: (0, i))
    border_spec = pl.BlockSpec((per_step, halves, MODES_TILE * SUBS, LANES), lambda i: (i, 0, 0, 0))
    conv, grad = pl.pallas_call(
        local_kernel,
        grid=(GROUPS,),
        in_specs=[signal_spec] * 4 + [mode_spec] * 2 + [border_spec] * 2,
        out_specs=[signal_spec] * 2,
        out_shape=[whole] * 2,
        scratch_shapes=[square] * 4,
        cost_estimate=cost(128, 24),
        name="local",
    )(*signals, rates, weight, before, after)
    gathered, conv, grad = lax.optimization_barrier((gathered, conv, grad))

    borders, part = pl.pallas_call(
        functools.partial(scan_kernel, tokens, blocks, 1.0 / (tokens * ctx_count * seq_count)),
        in_specs=[here] * 4,
        out_specs=[here] * 2,
        out_shape=[
            jax.ShapeDtypeStruct((ctx_count, 2 * MODES_TILE, LANES), F32),
            jax.ShapeDtypeStruct((seq_count, MODES_TILE, LANES), F32),
        ],
        compiler_params=small,
        name="scan",
    )(gathered, rates, weight, scaling)

    parts = lax.all_to_all(part, "seq", split_axis=0, concat_axis=0, tiled=True)
    repacked = pl.pallas_call(
        pack_kernel,
        in_specs=[here] * 2,
        out_specs=here,
        out_shape=jax.ShapeDtypeStruct((ctx_count, 3 * MODES_TILE, LANES), F32),
        compiler_params=small,
        name="pack",
    )(borders, parts)
    returned = lax.all_to_all(repacked, "ctx", split_axis=0, concat_axis=0, tiled=True)

    result = jax.ShapeDtypeStruct((tokens, channels), signal_type)
    *results, grad_rows = pl.pallas_call(
        output_kernel,
        in_specs=[here] * 5 + [there] * 2 + [here],
        out_specs=[there] * 5,
        out_shape=[result] * 4 + [jax.ShapeDtypeStruct((modes, channels), F32)],
        scratch_shapes=[pltpu.VMEM((modes, channels), F32)]
        + [pltpu.VMEM((tokens, channels), F32)] * 2
        + [signal_buffer] * 4
        + [pltpu.SemaphoreType.DMA((2, GROUPS)), pltpu.SemaphoreType.DMA((5, GROUPS))]
        + [pltpu.VMEM((tokens, channels), F32)] * 2,
        compiler_params=pltpu.CompilerParams(vmem_limit_bytes=OUTPUTS_VMEM),
        cost_estimate=cost(64, 24),
        name="outputs",
    )(*signals, rates, conv, grad, returned.reshape(halves, blocks, 3 * MODES_TILE, LANES))
    return (*[r[None] for r in results], grad_rows.T)


def solution(mesh):
    split = P("seq", "ctx", None)
    return jax.shard_map(
        on_device,
        mesh=mesh,
        in_specs=(split, split, split, split, P(), P()),
        out_specs=(split, split, split, split, P()),
        check_vma=False,
    )
```

```python
import functools

import jax
import jax.numpy as jnp
from jax import lax
from jax.experimental import pallas as pl
from jax.experimental.pallas import tpu as pltpu
from jax.sharding import PartitionSpec as P

LANES = 128
SUBS = 8
MODES_TILE = 8
F32 = jnp.float32
GROUPS = 4
STATE_GROUPS = 4
AHEAD = 2
PITCH = 17
EARLY_FLIPS = (1, 2)
LATE_FLIPS = (6,)
SMALL_VMEM = 12 * 1024 * 1024
STATES_VMEM = 58 * 1024 * 1024
OUTPUTS_VMEM = 51 * 1024 * 1024


def sub_index():
    return lax.broadcasted_iota(jnp.int32, (SUBS, LANES), 0)


def scale_of(rates):
    bent = jnp.tanh(rates)
    return jnp.sqrt(2.0 * bent / (1.0 + bent))


def rows_of(tile):
    return [jnp.broadcast_to(tile[m : m + 1], (SUBS, LANES)) for m in range(MODES_TILE)]


def states_kernel(
    query_hbm,
    key_hbm,
    value_hbm,
    cot_hbm,
    rates_hbm,
    packed_hbm,
    before_hbm,
    after_hbm,
    query_ref,
    key_ref,
    value_ref,
    cot_ref,
    rates_ref,
    packed_ref,
    before_ref,
    after_ref,
    rates_arrived,
    arrived,
    sent,
    u_ref,
    a_ref,
    lag_ref,
    lag_sum_ref,
    fwd_ref,
    bwd_ref,
):
    tokens, width = query_ref.shape
    steps = tokens // SUBS
    modes = rates_ref.shape[0]
    groups = arrived.shape[1]
    span = width // groups
    pairs = ((query_hbm, query_ref), (key_hbm, key_ref), (value_hbm, value_ref), (cot_hbm, cot_ref))

    def fetches(group):
        lanes = pl.ds(pl.multiple_of(group * span, span), span)
        return [
            pltpu.make_async_copy(source.at[:, lanes], target.at[:, lanes], arrived.at[n, group])
            for n, (source, target) in enumerate(pairs)
        ]

    def stores(group):
        count = span // LANES
        part = pl.ds(group * count, count)
        return [
            pltpu.make_async_copy(packed_ref.at[:, part], packed_hbm.at[:, part], sent.at[0, group]),
            pltpu.make_async_copy(before_ref.at[part], before_hbm.at[part], sent.at[1, group]),
            pltpu.make_async_copy(after_ref.at[part], after_hbm.at[part], sent.at[2, group]),
        ]

    rates_fetch = pltpu.make_async_copy(rates_hbm, rates_ref, rates_arrived)
    rates_fetch.start()
    for group in range(AHEAD):
        for fetch in fetches(group):
            fetch.start()
    rates_fetch.wait()

    def block(index, carry):
        lanes = pl.ds(pl.multiple_of(index * LANES, LANES), LANES)
        mixed = key_ref[:, lanes].astype(F32) * value_ref[:, lanes].astype(F32)
        adjoint = cot_ref[:, lanes].astype(F32) * query_ref[:, lanes].astype(F32)
        for s in range(SUBS):
            u_ref[s * PITCH : s * PITCH + steps, :] = mixed[s * steps : (s + 1) * steps]
            a_ref[s * PITCH : s * PITCH + steps, :] = adjoint[s * steps : (s + 1) * steps]
        u = [u_ref[pl.ds(i, SUBS, stride=PITCH), :] for i in range(steps)]
        a = [a_ref[pl.ds(i, SUBS, stride=PITCH), :] for i in range(steps)]
        for lag in range(steps):
            total = a[lag] * u[0]
            for i in range(1, steps - lag):
                total = total + a[lag + i] * u[i]
            lag_ref[lag * SUBS : (lag + 1) * SUBS, :] = total
        for group in range(steps // SUBS):
            total = None
            for s in range(SUBS):
                term = lag_ref[pl.ds(group * SUBS * SUBS + s, SUBS, stride=SUBS), :]
                total = term if total is None else total + term
            lag_sum_ref[group * SUBS : (group + 1) * SUBS, :] = total
        for half in range(modes // MODES_TILE):
            rates = rates_ref[half * MODES_TILE : (half + 1) * MODES_TILE, lanes]
            lam_tile = jnp.exp(-rates)
            lam = rows_of(lam_tile)
            fwd = [u_ref[pl.ds(0, SUBS, stride=PITCH), :]] * MODES_TILE
            bwd = [a_ref[pl.ds(steps - 1, SUBS, stride=PITCH), :]] * MODES_TILE
            for i in range(1, steps):
                front = u_ref[pl.ds(i, SUBS, stride=PITCH), :]
                back = a_ref[pl.ds(steps - 1 - i, SUBS, stride=PITCH), :]
                for m in range(MODES_TILE):
                    fwd[m] = lam[m] * fwd[m] + front
                    bwd[m] = lam[m] * bwd[m] + back
            for m in range(MODES_TILE):
                fwd_ref[m * SUBS : (m + 1) * SUBS, :] = fwd[m]
                bwd_ref[m * SUBS : (m + 1) * SUBS, :] = bwd[m]
            jump = jnp.exp(rates * -float(steps))
            zero = jnp.zeros((MODES_TILE, LANES), F32)
            before, after, cross, inner = zero, zero, zero, zero
            for s in range(SUBS):
                rows = pl.ds(s, MODES_TILE, stride=SUBS)
                before_ref[index, half, rows, :] = before
                cross = cross + bwd_ref[rows, :] * before
                before = jump * before + fwd_ref[rows, :]
            for s in reversed(range(SUBS)):
                rows = pl.ds(s, MODES_TILE, stride=SUBS)
                after_ref[index, half, rows, :] = after
                after = jump * after + bwd_ref[rows, :]
            for lag in reversed(range(steps)):
                inner = inner * lam_tile + lag_sum_ref[lag : lag + 1, :]
            packed_ref[half, index, 0:MODES_TILE, :] = before
            packed_ref[half, index, MODES_TILE : 2 * MODES_TILE, :] = after
            packed_ref[half, index, 2 * MODES_TILE : 3 * MODES_TILE, :] = inner + lam_tile * cross
        return carry

    def column(group, carry):
        for fetch in fetches(group):
            fetch.wait()

        @pl.when(group + AHEAD < groups)
        def _():
            for fetch in fetches(group + AHEAD):
                fetch.start()

        per_group = span // LANES
        carry = lax.fori_loop(0, per_group, lambda j, c: block(group * per_group + j, c), carry, unroll=True)
        for store in stores(group):
            store.start()
        return carry

    lax.fori_loop(0, groups, column, 0)
    for group in range(groups):
        for store in stores(group):
            store.wait()


def local_kernel(
    query_ref,
    key_ref,
    value_ref,
    cot_ref,
    rates_ref,
    residues_ref,
    before_ref,
    after_ref,
    conv_ref,
    grad_ref,
    u_ref,
    a_ref,
    y_ref,
    g_ref,
):
    tokens, width = query_ref.shape
    steps = tokens // SUBS
    modes = rates_ref.shape[0]

    def block(index, carry):
        lanes = pl.ds(pl.multiple_of(index * LANES, LANES), LANES)
        u_ref[...] = key_ref[:, lanes].astype(F32) * value_ref[:, lanes].astype(F32)
        a_ref[...] = cot_ref[:, lanes].astype(F32) * query_ref[:, lanes].astype(F32)
        for half in range(modes // MODES_TILE):
            picked = slice(half * MODES_TILE, (half + 1) * MODES_TILE)
            rates = rates_ref[picked, lanes]
            lam = rows_of(jnp.exp(-rates))
            weight = rows_of(residues_ref[picked, lanes] * scale_of(rates))
            fwd = [before_ref[index, half, m * SUBS : (m + 1) * SUBS, :] for m in range(MODES_TILE)]
            for i in range(steps):
                rows = pl.ds(i, SUBS, stride=steps)
                u = u_ref[rows, :]
                total = y_ref[rows, :] if half else None
                for m in range(MODES_TILE):
                    fwd[m] = lam[m] * fwd[m] + u
                    term = weight[m] * fwd[m]
                    total = term if total is None else total + term
                y_ref[rows, :] = total
            bwd = [after_ref[index, half, m * SUBS : (m + 1) * SUBS, :] for m in range(MODES_TILE)]
            for i in reversed(range(steps)):
                rows = pl.ds(i, SUBS, stride=steps)
                a = a_ref[rows, :]
                total = g_ref[rows, :] if half else None
                for m in range(MODES_TILE):
                    bwd[m] = lam[m] * bwd[m] + a
                    term = weight[m] * bwd[m]
                    total = term if total is None else total + term
                g_ref[rows, :] = total
        conv_ref[:, lanes] = y_ref[...]
        grad_ref[:, lanes] = g_ref[...]
        return carry

    lax.fori_loop(0, width // LANES, block, 0)


def scan_kernel(chunk_tokens, per_half, share, states_ref, rates_ref, residues_ref, out_ref, part_ref):
    chunks = states_ref.shape[0]
    rank = lax.axis_index("ctx")
    rows = pl.ds(pl.multiple_of((rank // per_half) * MODES_TILE, MODES_TILE), MODES_TILE)
    lanes = pl.ds(pl.multiple_of((rank % per_half) * LANES, LANES), LANES)
    rates = rates_ref[rows, lanes]
    lam = jnp.exp(-rates)
    jump = jnp.exp(rates * -float(chunk_tokens))
    scaling = scale_of(rates)
    entry = residues_ref[rows, lanes] * scaling * lam
    zero = jnp.zeros((MODES_TILE, LANES), F32)
    fwd, cross, inner = zero, zero, zero
    for j in range(chunks):
        out_ref[j, 0:MODES_TILE] = entry * fwd
        cross = cross + states_ref[j, MODES_TILE : 2 * MODES_TILE] * fwd
        inner = inner + states_ref[j, 2 * MODES_TILE : 3 * MODES_TILE]
        fwd = jump * fwd + states_ref[j, 0:MODES_TILE]
    bwd = zero
    for j in reversed(range(chunks)):
        out_ref[j, MODES_TILE : 2 * MODES_TILE] = entry * bwd
        bwd = jump * bwd + states_ref[j, MODES_TILE : 2 * MODES_TILE]
    part = (inner + lam * cross) * scaling * share
    part_ref[...] = part


def pack_kernel(states_ref, part_ref, out_ref):
    for j in range(out_ref.shape[0]):
        out_ref[j, 0 : 2 * MODES_TILE] = states_ref[j]
        out_ref[j, 2 * MODES_TILE : 3 * MODES_TILE] = part_ref[...]


def output_kernel(
    query_ref,
    key_ref,
    value_ref,
    cot_ref,
    rates_ref,
    conv_hbm,
    grad_hbm,
    entry_ref,
    out_hbm,
    grad_query_hbm,
    grad_key_hbm,
    grad_value_hbm,
    conv_ref,
    grad_ref,
    out_ref,
    grad_query_ref,
    grad_key_ref,
    grad_value_ref,
    arrived,
    sent,
    y_ref,
    g_ref,
):
    tokens, width = query_ref.shape
    modes = rates_ref.shape[0]
    groups = tokens // SUBS
    sub = sub_index().astype(F32)
    columns = sent.shape[1]
    span = width // columns
    pairs = (
        (out_ref, out_hbm),
        (grad_query_ref, grad_query_hbm),
        (grad_key_ref, grad_key_hbm),
        (grad_value_ref, grad_value_hbm),
    )

    inputs = (
        (conv_hbm, conv_ref),
        (grad_hbm, grad_ref),
    )

    def fetches(column):
        lanes = pl.ds(pl.multiple_of(column * span, span), span)
        return [
            pltpu.make_async_copy(source.at[:, lanes], target.at[:, lanes], arrived.at[n, column])
            for n, (source, target) in enumerate(inputs)
        ]

    for column in range(columns):
        for fetch in fetches(column):
            fetch.start()

    def stores(column):
        lanes = pl.ds(pl.multiple_of(column * span, span), span)
        return [
            pltpu.make_async_copy(source.at[:, lanes], target.at[:, lanes], sent.at[n, column])
            for n, (source, target) in enumerate(pairs)
        ]

    def entry(index, carry):
        lanes = pl.ds(pl.multiple_of(index * LANES, LANES), LANES)
        for half in range(modes // MODES_TILE):
            picked = slice(half * MODES_TILE, (half + 1) * MODES_TILE)
            rates = rates_ref[picked, lanes]
            row = rows_of(rates)
            jump = rows_of(jnp.exp(rates * -float(SUBS)))
            early = rows_of(entry_ref[half, index, 0:MODES_TILE, :])
            late = rows_of(entry_ref[half, index, MODES_TILE : 2 * MODES_TILE, :])
            fwd = [early[m] * jnp.exp(-row[m] * sub) for m in range(MODES_TILE)]
            bwd = [late[m] * jnp.exp(-row[m] * (SUBS - 1 - sub)) for m in range(MODES_TILE)]
            for i in range(groups):
                rows = slice(i * SUBS, (i + 1) * SUBS)
                total = y_ref[rows, lanes] if half else None
                for m in range(MODES_TILE):
                    total = fwd[m] if total is None else total + fwd[m]
                    fwd[m] = fwd[m] * jump[m]
                y_ref[rows, lanes] = total
                rows = slice((groups - 1 - i) * SUBS, (groups - i) * SUBS)
                total = g_ref[rows, lanes] if half else None
                for m in range(MODES_TILE):
                    total = bwd[m] if total is None else total + bwd[m]
                    bwd[m] = bwd[m] * jump[m]
                g_ref[rows, lanes] = total
        return carry

    def finish(index, carry):
        lanes = pl.ds(pl.multiple_of(index * LANES, LANES), LANES)
        y = y_ref[:, lanes] + conv_ref[:, lanes]
        g = g_ref[:, lanes] + grad_ref[:, lanes]
        out_ref[:, lanes] = (query_ref[:, lanes].astype(F32) * y).astype(out_ref.dtype)
        grad_query_ref[:, lanes] = (cot_ref[:, lanes].astype(F32) * y).astype(out_ref.dtype)
        grad_key_ref[:, lanes] = (value_ref[:, lanes].astype(F32) * g).astype(out_ref.dtype)
        grad_value_ref[:, lanes] = (key_ref[:, lanes].astype(F32) * g).astype(out_ref.dtype)
        return carry

    def column_step(column, carry):
        count = span // LANES
        carry = lax.fori_loop(0, count, lambda j, c: entry(column * count + j, c), carry, unroll=True)
        for fetch in fetches(column):
            fetch.wait()
        carry = lax.fori_loop(0, count, lambda j, c: finish(column * count + j, c), carry, unroll=True)
        for store in stores(column):
            store.start()
        return carry

    lax.fori_loop(0, columns, column_step, 0)
    for column in range(columns):
        for store in stores(column):
            store.wait()


def work(tokens, channels, ops, moved):
    return pl.CostEstimate(
        flops=ops * tokens * channels, bytes_accessed=moved * tokens * channels, transcendentals=0
    )


def states_call(signals, rates):
    tokens, channels = signals[0].shape
    modes = rates.shape[0]
    blocks = channels // LANES
    halves = modes // MODES_TILE
    there = pl.BlockSpec(memory_space=pltpu.HBM)
    border = jax.ShapeDtypeStruct((blocks, halves, MODES_TILE * SUBS, LANES), F32)
    square = pltpu.VMEM((tokens, LANES), F32)
    tile = pltpu.VMEM((MODES_TILE * SUBS, LANES), F32)
    signal_buffer = pltpu.VMEM((tokens, channels), signals[0].dtype)
    return pl.pallas_call(
        states_kernel,
        in_specs=[there] * 5,
        out_specs=[there] * 3,
        out_shape=[jax.ShapeDtypeStruct((halves, blocks, 3 * MODES_TILE, LANES), F32), border, border],
        scratch_shapes=[signal_buffer] * 4
        + [
            pltpu.VMEM((modes, channels), F32),
            pltpu.VMEM((halves, blocks, 3 * MODES_TILE, LANES), F32),
            pltpu.VMEM(border.shape, F32),
            pltpu.VMEM(border.shape, F32),
            pltpu.SemaphoreType.DMA(()),
            pltpu.SemaphoreType.DMA((4, STATE_GROUPS)),
            pltpu.SemaphoreType.DMA((3, STATE_GROUPS)),
            pltpu.VMEM((SUBS * PITCH, LANES), F32),
            pltpu.VMEM((SUBS * PITCH, LANES), F32),
            square,
            pltpu.VMEM((tokens // SUBS, LANES), F32),
            tile,
            tile,
        ],
        compiler_params=pltpu.CompilerParams(vmem_limit_bytes=STATES_VMEM),
        cost_estimate=work(tokens, channels, 96, 16),
        name="states",
    )(*signals, rates)


def seq_sum(tile, flips):
    for flip in flips:
        pairs = [(i, i ^ flip) for i in range(lax.axis_size("seq"))]
        tile = tile + lax.ppermute(tile, "seq", pairs)
    return tile


def on_device(query_input, key_input, value_input, cotangent, residues, decay_rates):
    tokens, channels = query_input.shape[1:]
    modes = residues.shape[1]
    ctx_count = lax.axis_size("ctx")
    seq_count = lax.axis_size("seq")
    blocks = channels // LANES
    halves = modes // MODES_TILE
    signals = [s[0] for s in (query_input, key_input, value_input, cotangent)]
    rates = decay_rates.T
    modal = residues.T

    here = pl.BlockSpec(memory_space=pltpu.VMEM)
    there = pl.BlockSpec(memory_space=pltpu.HBM)
    border = jax.ShapeDtypeStruct((blocks, halves, MODES_TILE * SUBS, LANES), F32)
    whole = jax.ShapeDtypeStruct((tokens, channels), F32)
    square = pltpu.VMEM((tokens, LANES), F32)
    signal_type = query_input.dtype
    signal_buffer = pltpu.VMEM((tokens, channels), signal_type)
    small = pltpu.CompilerParams(vmem_limit_bytes=SMALL_VMEM)

    packed, before, after = states_call(signals, rates)

    gathered = lax.all_to_all(
        packed.reshape(ctx_count, 3 * MODES_TILE, LANES), "ctx", split_axis=0, concat_axis=0, tiled=True
    )

    per_step = blocks // GROUPS
    signal_spec = pl.BlockSpec((tokens, per_step * LANES), lambda i: (0, i))
    mode_spec = pl.BlockSpec((modes, per_step * LANES), lambda i: (0, i))
    border_spec = pl.BlockSpec((per_step, halves, MODES_TILE * SUBS, LANES), lambda i: (i, 0, 0, 0))
    conv, grad = pl.pallas_call(
        local_kernel,
        grid=(GROUPS,),
        in_specs=[signal_spec] * 4 + [mode_spec] * 2 + [border_spec] * 2,
        out_specs=[signal_spec] * 2,
        out_shape=[whole] * 2,
        scratch_shapes=[square] * 4,
        cost_estimate=work(tokens, channels, 128, 24),
        name="local",
    )(*signals, rates, modal, before, after)
    gathered, conv, grad = lax.optimization_barrier((gathered, conv, grad))

    borders, part = pl.pallas_call(
        functools.partial(scan_kernel, tokens, blocks, 1.0 / (tokens * ctx_count * seq_count)),
        in_specs=[here] * 3,
        out_specs=[here] * 2,
        out_shape=[
            jax.ShapeDtypeStruct((ctx_count, 2 * MODES_TILE, LANES), F32),
            jax.ShapeDtypeStruct((MODES_TILE, LANES), F32),
        ],
        compiler_params=small,
        name="scan",
    )(gathered, rates, modal)

    part = seq_sum(part, EARLY_FLIPS)
    repacked = pl.pallas_call(
        pack_kernel,
        in_specs=[here] * 2,
        out_specs=here,
        out_shape=jax.ShapeDtypeStruct((ctx_count, 3 * MODES_TILE, LANES), F32),
        compiler_params=small,
        name="pack",
    )(borders, part)
    returned = lax.all_to_all(repacked, "ctx", split_axis=0, concat_axis=0, tiled=True)

    result = jax.ShapeDtypeStruct((tokens, channels), signal_type)
    results = pl.pallas_call(
        output_kernel,
        in_specs=[here] * 5 + [there] * 2 + [here],
        out_specs=[there] * 4,
        out_shape=[result] * 4,
        scratch_shapes=[pltpu.VMEM((tokens, channels), F32)] * 2
        + [signal_buffer] * 4
        + [pltpu.SemaphoreType.DMA((2, GROUPS)), pltpu.SemaphoreType.DMA((4, GROUPS))]
        + [pltpu.VMEM((tokens, channels), F32)] * 2,
        compiler_params=pltpu.CompilerParams(vmem_limit_bytes=OUTPUTS_VMEM),
        cost_estimate=work(tokens, channels, 64, 24),
        name="outputs",
    )(*signals, rates, conv, grad, returned.reshape(halves, blocks, 3 * MODES_TILE, LANES))
    tiles = seq_sum(returned[:, 2 * MODES_TILE :], LATE_FLIPS)
    grad_rows = tiles.reshape(halves, blocks, MODES_TILE, LANES).transpose(0, 2, 1, 3)
    return (*[r[None] for r in results], grad_rows.reshape(modes, channels).T)


def solution(mesh):
    split = P("seq", "ctx", None)
    return jax.shard_map(
        on_device,
        mesh=mesh,
        in_specs=(split, split, split, split, P(), P()),
        out_specs=(split, split, split, split, P()),
        check_vma=False,
    )
```

```python
import functools

import jax
import jax.numpy as jnp
from jax import lax
from jax.experimental import pallas as pl
from jax.experimental.pallas import tpu as pltpu
from jax.sharding import PartitionSpec as P

LANES = 128
SUBS = 8
MODES_TILE = 8
F32 = jnp.float32
GROUPS = 4
STATE_BLOCKS = (4, 4, 4, 4)
AHEAD = 2
UNROLL = 4
PITCH = 17
SMALL_VMEM = 12 * 1024 * 1024
STATES_VMEM = 58 * 1024 * 1024
OUTPUTS_VMEM = 51 * 1024 * 1024


def sub_index():
    return lax.broadcasted_iota(jnp.int32, (SUBS, LANES), 0)


def scale_of(rates):
    bent = jnp.tanh(rates)
    return jnp.sqrt(2.0 * bent / (1.0 + bent))


def rows_of(tile):
    return [jnp.broadcast_to(tile[m : m + 1], (SUBS, LANES)) for m in range(MODES_TILE)]


def states_kernel(
    query_hbm,
    key_hbm,
    value_hbm,
    cot_hbm,
    rates_hbm,
    packed_hbm,
    before_hbm,
    after_hbm,
    query_ref,
    key_ref,
    value_ref,
    cot_ref,
    rates_ref,
    packed_ref,
    before_ref,
    after_ref,
    rates_arrived,
    arrived,
    sent,
    u_ref,
    a_ref,
    lag_ref,
    lag_sum_ref,
    fwd_ref,
    bwd_ref,
):
    tokens, width = query_ref.shape
    steps = tokens // SUBS
    modes = rates_ref.shape[0]
    firsts = [sum(STATE_BLOCKS[:n]) for n in range(len(STATE_BLOCKS))]
    pairs = ((query_hbm, query_ref), (key_hbm, key_ref), (value_hbm, value_ref), (cot_hbm, cot_ref))

    def fetches(group):
        lanes = pl.ds(firsts[group] * LANES, STATE_BLOCKS[group] * LANES)
        return [
            pltpu.make_async_copy(source.at[:, lanes], target.at[:, lanes], arrived.at[n, group])
            for n, (source, target) in enumerate(pairs)
        ]

    def stores(group):
        part = pl.ds(firsts[group], STATE_BLOCKS[group])
        return [
            pltpu.make_async_copy(packed_ref.at[:, part], packed_hbm.at[:, part], sent.at[0, group]),
            pltpu.make_async_copy(before_ref.at[part], before_hbm.at[part], sent.at[1, group]),
            pltpu.make_async_copy(after_ref.at[part], after_hbm.at[part], sent.at[2, group]),
        ]

    rates_fetch = pltpu.make_async_copy(rates_hbm, rates_ref, rates_arrived)
    rates_fetch.start()
    for group in range(AHEAD):
        for fetch in fetches(group):
            fetch.start()
    rates_fetch.wait()

    def block(index, carry):
        lanes = pl.ds(pl.multiple_of(index * LANES, LANES), LANES)
        mixed = key_ref[:, lanes].astype(F32) * value_ref[:, lanes].astype(F32)
        adjoint = cot_ref[:, lanes].astype(F32) * query_ref[:, lanes].astype(F32)
        for s in range(SUBS):
            u_ref[s * PITCH : s * PITCH + steps, :] = mixed[s * steps : (s + 1) * steps]
            a_ref[s * PITCH : s * PITCH + steps, :] = adjoint[s * steps : (s + 1) * steps]
        u = [u_ref[pl.ds(i, SUBS, stride=PITCH), :] for i in range(steps)]
        a = [a_ref[pl.ds(i, SUBS, stride=PITCH), :] for i in range(steps)]
        for lag in range(steps):
            total = a[lag] * u[0]
            for i in range(1, steps - lag):
                total = total + a[lag + i] * u[i]
            lag_ref[lag * SUBS : (lag + 1) * SUBS, :] = total
        for group in range(steps // SUBS):
            total = None
            for s in range(SUBS):
                term = lag_ref[pl.ds(group * SUBS * SUBS + s, SUBS, stride=SUBS), :]
                total = term if total is None else total + term
            lag_sum_ref[group * SUBS : (group + 1) * SUBS, :] = total
        for half in range(modes // MODES_TILE):
            rates = rates_ref[half * MODES_TILE : (half + 1) * MODES_TILE, lanes]
            lam_tile = jnp.exp(-rates)
            lam = rows_of(lam_tile)
            fwd = [u_ref[pl.ds(0, SUBS, stride=PITCH), :]] * MODES_TILE
            bwd = [a_ref[pl.ds(steps - 1, SUBS, stride=PITCH), :]] * MODES_TILE
            for i in range(1, steps):
                front = u_ref[pl.ds(i, SUBS, stride=PITCH), :]
                back = a_ref[pl.ds(steps - 1 - i, SUBS, stride=PITCH), :]
                for m in range(MODES_TILE):
                    fwd[m] = lam[m] * fwd[m] + front
                    bwd[m] = lam[m] * bwd[m] + back
            for m in range(MODES_TILE):
                fwd_ref[m * SUBS : (m + 1) * SUBS, :] = fwd[m]
                bwd_ref[m * SUBS : (m + 1) * SUBS, :] = bwd[m]
            jump = jnp.exp(rates * -float(steps))
            zero = jnp.zeros((MODES_TILE, LANES), F32)
            before, after, cross, inner = zero, zero, zero, zero
            for s in range(SUBS):
                rows = pl.ds(s, MODES_TILE, stride=SUBS)
                before_ref[index, half, rows, :] = before
                cross = cross + bwd_ref[rows, :] * before
                before = jump * before + fwd_ref[rows, :]
            for s in reversed(range(SUBS)):
                rows = pl.ds(s, MODES_TILE, stride=SUBS)
                after_ref[index, half, rows, :] = after
                after = jump * after + bwd_ref[rows, :]
            for lag in reversed(range(steps)):
                inner = inner * lam_tile + lag_sum_ref[lag : lag + 1, :]
            packed_ref[half, index, 0:MODES_TILE, :] = before
            packed_ref[half, index, MODES_TILE : 2 * MODES_TILE, :] = after
            packed_ref[half, index, 2 * MODES_TILE : 3 * MODES_TILE, :] = inner + lam_tile * cross
        return carry

    for group, (first, count) in enumerate(zip(firsts, STATE_BLOCKS, strict=True)):
        for fetch in fetches(group):
            fetch.wait()
        if group + AHEAD < len(firsts):
            for fetch in fetches(group + AHEAD):
                fetch.start()
        if UNROLL >= count:
            for index in range(first, first + count):
                block(index, 0)
        else:
            lax.fori_loop(first, first + count, block, 0, unroll=UNROLL)
        for store in stores(group):
            store.start()
    for group in range(len(firsts)):
        for store in stores(group):
            store.wait()


def local_kernel(
    query_ref,
    key_ref,
    value_ref,
    cot_ref,
    rates_ref,
    residues_ref,
    before_ref,
    after_ref,
    conv_ref,
    grad_ref,
    u_ref,
    a_ref,
    y_ref,
    g_ref,
):
    tokens, width = query_ref.shape
    steps = tokens // SUBS
    modes = rates_ref.shape[0]

    def block(index, carry):
        lanes = pl.ds(pl.multiple_of(index * LANES, LANES), LANES)
        u_ref[...] = key_ref[:, lanes].astype(F32) * value_ref[:, lanes].astype(F32)
        a_ref[...] = cot_ref[:, lanes].astype(F32) * query_ref[:, lanes].astype(F32)
        for half in range(modes // MODES_TILE):
            picked = slice(half * MODES_TILE, (half + 1) * MODES_TILE)
            rates = rates_ref[picked, lanes]
            lam = rows_of(jnp.exp(-rates))
            weight = rows_of(residues_ref[picked, lanes] * scale_of(rates))
            fwd = [before_ref[index, half, m * SUBS : (m + 1) * SUBS, :] for m in range(MODES_TILE)]
            for i in range(steps):
                rows = pl.ds(i, SUBS, stride=steps)
                u = u_ref[rows, :]
                total = y_ref[rows, :] if half else None
                for m in range(MODES_TILE):
                    fwd[m] = lam[m] * fwd[m] + u
                    term = weight[m] * fwd[m]
                    total = term if total is None else total + term
                y_ref[rows, :] = total
            bwd = [after_ref[index, half, m * SUBS : (m + 1) * SUBS, :] for m in range(MODES_TILE)]
            for i in reversed(range(steps)):
                rows = pl.ds(i, SUBS, stride=steps)
                a = a_ref[rows, :]
                total = g_ref[rows, :] if half else None
                for m in range(MODES_TILE):
                    bwd[m] = lam[m] * bwd[m] + a
                    term = weight[m] * bwd[m]
                    total = term if total is None else total + term
                g_ref[rows, :] = total
        conv_ref[:, lanes] = y_ref[...]
        grad_ref[:, lanes] = g_ref[...]
        return carry

    lax.fori_loop(0, width // LANES, block, 0)


def scan_kernel(chunk_tokens, per_half, share, states_ref, rates_ref, residues_ref, out_ref, part_ref):
    chunks = states_ref.shape[0]
    rank = lax.axis_index("ctx")
    rows = pl.ds(pl.multiple_of((rank // per_half) * MODES_TILE, MODES_TILE), MODES_TILE)
    lanes = pl.ds(pl.multiple_of((rank % per_half) * LANES, LANES), LANES)
    rates = rates_ref[rows, lanes]
    lam = jnp.exp(-rates)
    jump = jnp.exp(rates * -float(chunk_tokens))
    scaling = scale_of(rates)
    entry = residues_ref[rows, lanes] * scaling * lam
    zero = jnp.zeros((MODES_TILE, LANES), F32)
    fwd, cross, inner = zero, zero, zero
    for j in range(chunks):
        out_ref[j, 0:MODES_TILE] = entry * fwd
        cross = cross + states_ref[j, MODES_TILE : 2 * MODES_TILE] * fwd
        inner = inner + states_ref[j, 2 * MODES_TILE : 3 * MODES_TILE]
        fwd = jump * fwd + states_ref[j, 0:MODES_TILE]
    bwd = zero
    for j in reversed(range(chunks)):
        out_ref[j, MODES_TILE : 2 * MODES_TILE] = entry * bwd
        bwd = jump * bwd + states_ref[j, MODES_TILE : 2 * MODES_TILE]
    part = (inner + lam * cross) * scaling * share
    part_ref[...] = part


def pack_kernel(states_ref, part_ref, out_ref):
    for j in range(out_ref.shape[0]):
        out_ref[j, 0 : 2 * MODES_TILE] = states_ref[j]
        out_ref[j, 2 * MODES_TILE : 3 * MODES_TILE] = part_ref[...]


def output_kernel(
    query_ref,
    key_ref,
    value_ref,
    cot_ref,
    rates_ref,
    conv_hbm,
    grad_hbm,
    entry_ref,
    out_hbm,
    grad_query_hbm,
    grad_key_hbm,
    grad_value_hbm,
    conv_ref,
    grad_ref,
    out_ref,
    grad_query_ref,
    grad_key_ref,
    grad_value_ref,
    arrived,
    sent,
    y_ref,
    g_ref,
):
    tokens, width = query_ref.shape
    modes = rates_ref.shape[0]
    groups = tokens // SUBS
    sub = sub_index().astype(F32)
    columns = sent.shape[1]
    span = width // columns
    pairs = (
        (out_ref, out_hbm),
        (grad_query_ref, grad_query_hbm),
        (grad_key_ref, grad_key_hbm),
        (grad_value_ref, grad_value_hbm),
    )

    inputs = (
        (conv_hbm, conv_ref),
        (grad_hbm, grad_ref),
    )

    def fetches(column):
        lanes = pl.ds(pl.multiple_of(column * span, span), span)
        return [
            pltpu.make_async_copy(source.at[:, lanes], target.at[:, lanes], arrived.at[n, column])
            for n, (source, target) in enumerate(inputs)
        ]

    for column in range(columns):
        for fetch in fetches(column):
            fetch.start()

    def stores(column):
        lanes = pl.ds(pl.multiple_of(column * span, span), span)
        return [
            pltpu.make_async_copy(source.at[:, lanes], target.at[:, lanes], sent.at[n, column])
            for n, (source, target) in enumerate(pairs)
        ]

    def entry(index, carry):
        lanes = pl.ds(pl.multiple_of(index * LANES, LANES), LANES)
        for half in range(modes // MODES_TILE):
            picked = slice(half * MODES_TILE, (half + 1) * MODES_TILE)
            rates = rates_ref[picked, lanes]
            row = rows_of(rates)
            jump = rows_of(jnp.exp(rates * -float(SUBS)))
            early = rows_of(entry_ref[half, index, 0:MODES_TILE, :])
            late = rows_of(entry_ref[half, index, MODES_TILE : 2 * MODES_TILE, :])
            fwd = [early[m] * jnp.exp(-row[m] * sub) for m in range(MODES_TILE)]
            bwd = [late[m] * jnp.exp(-row[m] * (SUBS - 1 - sub)) for m in range(MODES_TILE)]
            for i in range(groups):
                rows = slice(i * SUBS, (i + 1) * SUBS)
                total = y_ref[rows, lanes] if half else None
                for m in range(MODES_TILE):
                    total = fwd[m] if total is None else total + fwd[m]
                    fwd[m] = fwd[m] * jump[m]
                y_ref[rows, lanes] = total
                rows = slice((groups - 1 - i) * SUBS, (groups - i) * SUBS)
                total = g_ref[rows, lanes] if half else None
                for m in range(MODES_TILE):
                    total = bwd[m] if total is None else total + bwd[m]
                    bwd[m] = bwd[m] * jump[m]
                g_ref[rows, lanes] = total
        return carry

    def finish(index, carry):
        lanes = pl.ds(pl.multiple_of(index * LANES, LANES), LANES)
        y = y_ref[:, lanes] + conv_ref[:, lanes]
        g = g_ref[:, lanes] + grad_ref[:, lanes]
        out_ref[:, lanes] = (query_ref[:, lanes].astype(F32) * y).astype(out_ref.dtype)
        grad_query_ref[:, lanes] = (cot_ref[:, lanes].astype(F32) * y).astype(out_ref.dtype)
        grad_key_ref[:, lanes] = (value_ref[:, lanes].astype(F32) * g).astype(out_ref.dtype)
        grad_value_ref[:, lanes] = (key_ref[:, lanes].astype(F32) * g).astype(out_ref.dtype)
        return carry

    def column_step(column, carry):
        count = span // LANES
        carry = lax.fori_loop(0, count, lambda j, c: entry(column * count + j, c), carry, unroll=True)
        for fetch in fetches(column):
            fetch.wait()
        carry = lax.fori_loop(0, count, lambda j, c: finish(column * count + j, c), carry, unroll=True)
        for store in stores(column):
            store.start()
        return carry

    lax.fori_loop(0, columns, column_step, 0)
    for column in range(columns):
        for store in stores(column):
            store.wait()


def work(tokens, channels, ops, moved):
    return pl.CostEstimate(
        flops=ops * tokens * channels, bytes_accessed=moved * tokens * channels, transcendentals=0
    )


def states_call(signals, rates):
    tokens, channels = signals[0].shape
    modes = rates.shape[0]
    blocks = channels // LANES
    halves = modes // MODES_TILE
    there = pl.BlockSpec(memory_space=pltpu.HBM)
    border = jax.ShapeDtypeStruct((blocks, halves, MODES_TILE * SUBS, LANES), F32)
    square = pltpu.VMEM((tokens, LANES), F32)
    tile = pltpu.VMEM((MODES_TILE * SUBS, LANES), F32)
    signal_buffer = pltpu.VMEM((tokens, channels), signals[0].dtype)
    return pl.pallas_call(
        states_kernel,
        in_specs=[there] * 5,
        out_specs=[there] * 3,
        out_shape=[jax.ShapeDtypeStruct((halves, blocks, 3 * MODES_TILE, LANES), F32), border, border],
        scratch_shapes=[signal_buffer] * 4
        + [
            pltpu.VMEM((modes, channels), F32),
            pltpu.VMEM((halves, blocks, 3 * MODES_TILE, LANES), F32),
            pltpu.VMEM(border.shape, F32),
            pltpu.VMEM(border.shape, F32),
            pltpu.SemaphoreType.DMA(()),
            pltpu.SemaphoreType.DMA((4, len(STATE_BLOCKS))),
            pltpu.SemaphoreType.DMA((3, len(STATE_BLOCKS))),
            pltpu.VMEM((SUBS * PITCH, LANES), F32),
            pltpu.VMEM((SUBS * PITCH, LANES), F32),
            square,
            pltpu.VMEM((tokens // SUBS, LANES), F32),
            tile,
            tile,
        ],
        compiler_params=pltpu.CompilerParams(vmem_limit_bytes=STATES_VMEM),
        cost_estimate=work(tokens, channels, 96, 16),
        name="states",
    )(*signals, rates)


def outputs_call(signals, rates, conv, grad, entries):
    tokens, channels = signals[0].shape
    signal_type = signals[0].dtype
    signal_buffer = pltpu.VMEM((tokens, channels), signal_type)
    here = pl.BlockSpec(memory_space=pltpu.VMEM)
    there = pl.BlockSpec(memory_space=pltpu.HBM)
    result = jax.ShapeDtypeStruct((tokens, channels), signal_type)
    return pl.pallas_call(
        output_kernel,
        in_specs=[here] * 5 + [there] * 2 + [here],
        out_specs=[there] * 4,
        out_shape=[result] * 4,
        scratch_shapes=[pltpu.VMEM((tokens, channels), F32)] * 2
        + [signal_buffer] * 4
        + [pltpu.SemaphoreType.DMA((2, GROUPS)), pltpu.SemaphoreType.DMA((4, GROUPS))]
        + [pltpu.VMEM((tokens, channels), F32)] * 2,
        compiler_params=pltpu.CompilerParams(vmem_limit_bytes=OUTPUTS_VMEM),
        cost_estimate=work(tokens, channels, 64, 24),
        name="outputs",
    )(*signals, rates, conv, grad, entries)


def on_device(query_input, key_input, value_input, cotangent, residues, decay_rates):
    tokens, channels = query_input.shape[1:]
    modes = residues.shape[1]
    ctx_count = lax.axis_size("ctx")
    seq_count = lax.axis_size("seq")
    blocks = channels // LANES
    halves = modes // MODES_TILE
    signals = [s[0] for s in (query_input, key_input, value_input, cotangent)]
    rates = decay_rates.T
    modal = residues.T

    here = pl.BlockSpec(memory_space=pltpu.VMEM)
    whole = jax.ShapeDtypeStruct((tokens, channels), F32)
    square = pltpu.VMEM((tokens, LANES), F32)
    small = pltpu.CompilerParams(vmem_limit_bytes=SMALL_VMEM)

    packed, before, after = states_call(signals, rates)

    gathered = lax.all_to_all(
        packed.reshape(ctx_count, 3 * MODES_TILE, LANES), "ctx", split_axis=0, concat_axis=0, tiled=True
    )

    per_step = blocks // GROUPS
    signal_spec = pl.BlockSpec((tokens, per_step * LANES), lambda i: (0, i))
    mode_spec = pl.BlockSpec((modes, per_step * LANES), lambda i: (0, i))
    border_spec = pl.BlockSpec((per_step, halves, MODES_TILE * SUBS, LANES), lambda i: (i, 0, 0, 0))
    conv, grad = pl.pallas_call(
        local_kernel,
        grid=(GROUPS,),
        in_specs=[signal_spec] * 4 + [mode_spec] * 2 + [border_spec] * 2,
        out_specs=[signal_spec] * 2,
        out_shape=[whole] * 2,
        scratch_shapes=[square] * 4,
        cost_estimate=work(tokens, channels, 128, 24),
        name="local",
    )(*signals, rates, modal, before, after)
    gathered, conv, grad = lax.optimization_barrier((gathered, conv, grad))

    borders, part = pl.pallas_call(
        functools.partial(scan_kernel, tokens, blocks, 1.0 / (tokens * ctx_count * seq_count)),
        in_specs=[here] * 3,
        out_specs=[here] * 2,
        out_shape=[
            jax.ShapeDtypeStruct((ctx_count, 2 * MODES_TILE, LANES), F32),
            jax.ShapeDtypeStruct((MODES_TILE, LANES), F32),
        ],
        compiler_params=small,
        name="scan",
    )(gathered, rates, modal)

    near, far, cross = (
        lax.ppermute(part, "seq", [(i, i ^ flip) for i in range(seq_count)]) for flip in (1, 2, 3)
    )
    part = (part + near) + (far + cross)
    repacked = pl.pallas_call(
        pack_kernel,
        in_specs=[here] * 2,
        out_specs=here,
        out_shape=jax.ShapeDtypeStruct((ctx_count, 3 * MODES_TILE, LANES), F32),
        compiler_params=small,
        name="pack",
    )(borders, part)
    returned = lax.all_to_all(repacked, "ctx", split_axis=0, concat_axis=0, tiled=True)

    entries = returned.reshape(halves, blocks, 3 * MODES_TILE, LANES)
    results = outputs_call(signals, rates, conv, grad, entries)
    tiles = returned[:, 2 * MODES_TILE :]
    tiles = tiles + lax.ppermute(tiles, "seq", [(i, i ^ 6) for i in range(seq_count)])
    grad_rows = tiles.reshape(halves, blocks, MODES_TILE, LANES).transpose(0, 2, 1, 3)
    return (*[r[None] for r in results], grad_rows.reshape(modes, channels).T)


def solution(mesh):
    split = P("seq", "ctx", None)
    return jax.shard_map(
        on_device,
        mesh=mesh,
        in_specs=(split, split, split, split, P(), P()),
        out_specs=(split, split, split, split, P()),
        check_vma=False,
    )
```

```python
import functools

import jax
import jax.numpy as jnp
from jax import lax
from jax.experimental import pallas as pl
from jax.experimental.pallas import tpu as pltpu
from jax.sharding import PartitionSpec as P

LANES = 128
SUBS = 8
MODES_TILE = 8
F32 = jnp.float32
GROUPS = 4
OUTPUT_COLUMNS = 2
STATE_BLOCKS = (4, 4, 4, 4)
AHEAD = 2
UNROLL = 4
PITCH = 17
SMALL_VMEM = 12 * 1024 * 1024
STATES_VMEM = 58 * 1024 * 1024
OUTPUTS_VMEM = 51 * 1024 * 1024


def sub_index():
    return lax.broadcasted_iota(jnp.int32, (SUBS, LANES), 0)


def scale_of(rates):
    bent = jnp.tanh(rates)
    return jnp.sqrt(2.0 * bent / (1.0 + bent))


def rows_of(tile):
    return [jnp.broadcast_to(tile[m : m + 1], (SUBS, LANES)) for m in range(MODES_TILE)]


def states_kernel(
    query_hbm,
    key_hbm,
    value_hbm,
    cot_hbm,
    rates_hbm,
    packed_hbm,
    before_hbm,
    after_hbm,
    query_ref,
    key_ref,
    value_ref,
    cot_ref,
    rates_ref,
    packed_ref,
    before_ref,
    after_ref,
    rates_arrived,
    arrived,
    sent,
    u_ref,
    a_ref,
    lag_ref,
    lag_sum_ref,
    fwd_ref,
    bwd_ref,
):
    tokens, width = query_ref.shape
    steps = tokens // SUBS
    modes = rates_ref.shape[0]
    firsts = [sum(STATE_BLOCKS[:n]) for n in range(len(STATE_BLOCKS))]
    pairs = ((query_hbm, query_ref), (key_hbm, key_ref), (value_hbm, value_ref), (cot_hbm, cot_ref))

    def fetches(group):
        lanes = pl.ds(firsts[group] * LANES, STATE_BLOCKS[group] * LANES)
        return [
            pltpu.make_async_copy(source.at[:, lanes], target.at[:, lanes], arrived.at[n, group])
            for n, (source, target) in enumerate(pairs)
        ]

    def stores(group):
        part = pl.ds(firsts[group], STATE_BLOCKS[group])
        return [
            pltpu.make_async_copy(packed_ref.at[:, part], packed_hbm.at[:, part], sent.at[0, group]),
            pltpu.make_async_copy(before_ref.at[part], before_hbm.at[part], sent.at[1, group]),
            pltpu.make_async_copy(after_ref.at[part], after_hbm.at[part], sent.at[2, group]),
        ]

    rates_fetch = pltpu.make_async_copy(rates_hbm, rates_ref, rates_arrived)
    rates_fetch.start()
    for group in range(AHEAD):
        for fetch in fetches(group):
            fetch.start()
    rates_fetch.wait()

    def block(index, carry):
        lanes = pl.ds(pl.multiple_of(index * LANES, LANES), LANES)
        mixed = key_ref[:, lanes].astype(F32) * value_ref[:, lanes].astype(F32)
        adjoint = cot_ref[:, lanes].astype(F32) * query_ref[:, lanes].astype(F32)
        for s in range(SUBS):
            u_ref[s * PITCH : s * PITCH + steps, :] = mixed[s * steps : (s + 1) * steps]
            a_ref[s * PITCH : s * PITCH + steps, :] = adjoint[s * steps : (s + 1) * steps]
        u = [u_ref[pl.ds(i, SUBS, stride=PITCH), :] for i in range(steps)]
        a = [a_ref[pl.ds(i, SUBS, stride=PITCH), :] for i in range(steps)]
        for lag in range(steps):
            total = a[lag] * u[0]
            for i in range(1, steps - lag):
                total = total + a[lag + i] * u[i]
            lag_ref[lag * SUBS : (lag + 1) * SUBS, :] = total
        for group in range(steps // SUBS):
            total = None
            for s in range(SUBS):
                term = lag_ref[pl.ds(group * SUBS * SUBS + s, SUBS, stride=SUBS), :]
                total = term if total is None else total + term
            lag_sum_ref[group * SUBS : (group + 1) * SUBS, :] = total
        for half in range(modes // MODES_TILE):
            rates = rates_ref[half * MODES_TILE : (half + 1) * MODES_TILE, lanes]
            lam_tile = jnp.exp(-rates)
            lam = rows_of(lam_tile)
            fwd = [u_ref[pl.ds(0, SUBS, stride=PITCH), :]] * MODES_TILE
            bwd = [a_ref[pl.ds(steps - 1, SUBS, stride=PITCH), :]] * MODES_TILE
            for i in range(1, steps):
                front = u_ref[pl.ds(i, SUBS, stride=PITCH), :]
                back = a_ref[pl.ds(steps - 1 - i, SUBS, stride=PITCH), :]
                for m in range(MODES_TILE):
                    fwd[m] = lam[m] * fwd[m] + front
                    bwd[m] = lam[m] * bwd[m] + back
            for m in range(MODES_TILE):
                fwd_ref[m * SUBS : (m + 1) * SUBS, :] = fwd[m]
                bwd_ref[m * SUBS : (m + 1) * SUBS, :] = bwd[m]
            jump = jnp.exp(rates * -float(steps))
            zero = jnp.zeros((MODES_TILE, LANES), F32)
            before, after, cross, inner = zero, zero, zero, zero
            for s in range(SUBS):
                rows = pl.ds(s, MODES_TILE, stride=SUBS)
                before_ref[index, half, rows, :] = before
                cross = cross + bwd_ref[rows, :] * before
                before = jump * before + fwd_ref[rows, :]
            for s in reversed(range(SUBS)):
                rows = pl.ds(s, MODES_TILE, stride=SUBS)
                after_ref[index, half, rows, :] = after
                after = jump * after + bwd_ref[rows, :]
            for lag in reversed(range(steps)):
                inner = inner * lam_tile + lag_sum_ref[lag : lag + 1, :]
            packed_ref[half, index, 0:MODES_TILE, :] = before
            packed_ref[half, index, MODES_TILE : 2 * MODES_TILE, :] = after
            packed_ref[half, index, 2 * MODES_TILE : 3 * MODES_TILE, :] = inner + lam_tile * cross
        return carry

    for group, (first, count) in enumerate(zip(firsts, STATE_BLOCKS, strict=True)):
        for fetch in fetches(group):
            fetch.wait()
        if group + AHEAD < len(firsts):
            for fetch in fetches(group + AHEAD):
                fetch.start()
        if UNROLL >= count:
            for index in range(first, first + count):
                block(index, 0)
        else:
            lax.fori_loop(first, first + count, block, 0, unroll=UNROLL)
        for store in stores(group):
            store.start()
    for group in range(len(firsts)):
        for store in stores(group):
            store.wait()


def local_kernel(
    query_ref,
    key_ref,
    value_ref,
    cot_ref,
    rates_ref,
    residues_ref,
    before_ref,
    after_ref,
    conv_ref,
    grad_ref,
    u_ref,
    a_ref,
    y_ref,
    g_ref,
):
    tokens, width = query_ref.shape
    steps = tokens // SUBS
    modes = rates_ref.shape[0]

    def block(index, carry):
        lanes = pl.ds(pl.multiple_of(index * LANES, LANES), LANES)
        u_ref[...] = key_ref[:, lanes].astype(F32) * value_ref[:, lanes].astype(F32)
        a_ref[...] = cot_ref[:, lanes].astype(F32) * query_ref[:, lanes].astype(F32)
        for half in range(modes // MODES_TILE):
            picked = slice(half * MODES_TILE, (half + 1) * MODES_TILE)
            rates = rates_ref[picked, lanes]
            lam = rows_of(jnp.exp(-rates))
            weight = rows_of(residues_ref[picked, lanes] * scale_of(rates))
            fwd = [before_ref[index, half, m * SUBS : (m + 1) * SUBS, :] for m in range(MODES_TILE)]
            for i in range(steps):
                rows = pl.ds(i, SUBS, stride=steps)
                u = u_ref[rows, :]
                total = y_ref[rows, :] if half else None
                for m in range(MODES_TILE):
                    fwd[m] = lam[m] * fwd[m] + u
                    term = weight[m] * fwd[m]
                    total = term if total is None else total + term
                y_ref[rows, :] = total
            bwd = [after_ref[index, half, m * SUBS : (m + 1) * SUBS, :] for m in range(MODES_TILE)]
            for i in reversed(range(steps)):
                rows = pl.ds(i, SUBS, stride=steps)
                a = a_ref[rows, :]
                total = g_ref[rows, :] if half else None
                for m in range(MODES_TILE):
                    bwd[m] = lam[m] * bwd[m] + a
                    term = weight[m] * bwd[m]
                    total = term if total is None else total + term
                g_ref[rows, :] = total
        conv_ref[:, lanes] = y_ref[...]
        grad_ref[:, lanes] = g_ref[...]
        return carry

    lax.fori_loop(0, width // LANES, block, 0)


def scan_kernel(chunk_tokens, per_half, share, states_ref, rates_ref, residues_ref, out_ref, part_ref):
    chunks = states_ref.shape[0]
    rank = lax.axis_index("ctx")
    rows = pl.ds(pl.multiple_of((rank // per_half) * MODES_TILE, MODES_TILE), MODES_TILE)
    lanes = pl.ds(pl.multiple_of((rank % per_half) * LANES, LANES), LANES)
    rates = rates_ref[rows, lanes]
    lam = jnp.exp(-rates)
    jump = jnp.exp(rates * -float(chunk_tokens))
    scaling = scale_of(rates)
    entry = residues_ref[rows, lanes] * scaling * lam
    zero = jnp.zeros((MODES_TILE, LANES), F32)
    fwd, cross, inner = zero, zero, zero
    for j in range(chunks):
        out_ref[j, 0:MODES_TILE] = entry * fwd
        cross = cross + states_ref[j, MODES_TILE : 2 * MODES_TILE] * fwd
        inner = inner + states_ref[j, 2 * MODES_TILE : 3 * MODES_TILE]
        fwd = jump * fwd + states_ref[j, 0:MODES_TILE]
    bwd = zero
    for j in reversed(range(chunks)):
        out_ref[j, MODES_TILE : 2 * MODES_TILE] = entry * bwd
        bwd = jump * bwd + states_ref[j, MODES_TILE : 2 * MODES_TILE]
    part = (inner + lam * cross) * scaling * share
    part_ref[...] = part


def pack_kernel(states_ref, part_ref, out_ref):
    for j in range(out_ref.shape[0]):
        out_ref[j, 0 : 2 * MODES_TILE] = states_ref[j]
        out_ref[j, 2 * MODES_TILE : 3 * MODES_TILE] = part_ref[...]


def output_kernel(
    query_ref,
    key_ref,
    value_ref,
    cot_ref,
    rates_ref,
    conv_hbm,
    grad_hbm,
    entry_ref,
    out_hbm,
    grad_query_hbm,
    grad_key_hbm,
    grad_value_hbm,
    conv_ref,
    grad_ref,
    out_ref,
    grad_query_ref,
    grad_key_ref,
    grad_value_ref,
    arrived,
    sent,
    y_ref,
    g_ref,
):
    tokens, width = query_ref.shape
    modes = rates_ref.shape[0]
    groups = tokens // SUBS
    sub = sub_index().astype(F32)
    columns = sent.shape[1]
    span = width // columns
    pairs = (
        (out_ref, out_hbm),
        (grad_query_ref, grad_query_hbm),
        (grad_key_ref, grad_key_hbm),
        (grad_value_ref, grad_value_hbm),
    )

    inputs = (
        (conv_hbm, conv_ref),
        (grad_hbm, grad_ref),
    )

    def fetches(column):
        lanes = pl.ds(column * span, span)
        return [
            pltpu.make_async_copy(source.at[:, lanes], target.at[:, lanes], arrived.at[n, column])
            for n, (source, target) in enumerate(inputs)
        ]

    for column in range(columns):
        for fetch in fetches(column):
            fetch.start()

    def stores(column):
        lanes = pl.ds(column * span, span)
        return [
            pltpu.make_async_copy(source.at[:, lanes], target.at[:, lanes], sent.at[n, column])
            for n, (source, target) in enumerate(pairs)
        ]

    def entry(index, carry):
        lanes = pl.ds(pl.multiple_of(index * LANES, LANES), LANES)
        for half in range(modes // MODES_TILE):
            picked = slice(half * MODES_TILE, (half + 1) * MODES_TILE)
            rates = rates_ref[picked, lanes]
            row = rows_of(rates)
            jump = rows_of(jnp.exp(rates * -float(SUBS)))
            early = rows_of(entry_ref[half, index, 0:MODES_TILE, :])
            late = rows_of(entry_ref[half, index, MODES_TILE : 2 * MODES_TILE, :])
            fwd = [early[m] * jnp.exp(-row[m] * sub) for m in range(MODES_TILE)]
            bwd = [late[m] * jnp.exp(-row[m] * (SUBS - 1 - sub)) for m in range(MODES_TILE)]
            for i in range(groups):
                rows = slice(i * SUBS, (i + 1) * SUBS)
                total = y_ref[rows, lanes] if half else None
                for m in range(MODES_TILE):
                    total = fwd[m] if total is None else total + fwd[m]
                    fwd[m] = fwd[m] * jump[m]
                y_ref[rows, lanes] = total
                rows = slice((groups - 1 - i) * SUBS, (groups - i) * SUBS)
                total = g_ref[rows, lanes] if half else None
                for m in range(MODES_TILE):
                    total = bwd[m] if total is None else total + bwd[m]
                    bwd[m] = bwd[m] * jump[m]
                g_ref[rows, lanes] = total
        return carry

    def finish(index, carry):
        lanes = pl.ds(pl.multiple_of(index * LANES, LANES), LANES)
        y = y_ref[:, lanes] + conv_ref[:, lanes]
        g = g_ref[:, lanes] + grad_ref[:, lanes]
        out_ref[:, lanes] = (query_ref[:, lanes].astype(F32) * y).astype(out_ref.dtype)
        grad_query_ref[:, lanes] = (cot_ref[:, lanes].astype(F32) * y).astype(out_ref.dtype)
        grad_key_ref[:, lanes] = (value_ref[:, lanes].astype(F32) * g).astype(out_ref.dtype)
        grad_value_ref[:, lanes] = (key_ref[:, lanes].astype(F32) * g).astype(out_ref.dtype)
        return carry

    count = span // LANES
    for column in range(columns):
        first = column * count
        lax.fori_loop(first, first + count, entry, 0, unroll=True)
        for fetch in fetches(column):
            fetch.wait()
        lax.fori_loop(first, first + count, finish, 0, unroll=True)
        for store in stores(column):
            store.start()
    for column in range(columns):
        for store in stores(column):
            store.wait()


def work(tokens, channels, ops, moved):
    return pl.CostEstimate(
        flops=ops * tokens * channels, bytes_accessed=moved * tokens * channels, transcendentals=0
    )


def states_call(signals, rates):
    tokens, channels = signals[0].shape
    modes = rates.shape[0]
    blocks = channels // LANES
    halves = modes // MODES_TILE
    there = pl.BlockSpec(memory_space=pltpu.HBM)
    border = jax.ShapeDtypeStruct((blocks, halves, MODES_TILE * SUBS, LANES), F32)
    square = pltpu.VMEM((tokens, LANES), F32)
    tile = pltpu.VMEM((MODES_TILE * SUBS, LANES), F32)
    signal_buffer = pltpu.VMEM((tokens, channels), signals[0].dtype)
    return pl.pallas_call(
        states_kernel,
        in_specs=[there] * 5,
        out_specs=[there] * 3,
        out_shape=[jax.ShapeDtypeStruct((halves, blocks, 3 * MODES_TILE, LANES), F32), border, border],
        scratch_shapes=[signal_buffer] * 4
        + [
            pltpu.VMEM((modes, channels), F32),
            pltpu.VMEM((halves, blocks, 3 * MODES_TILE, LANES), F32),
            pltpu.VMEM(border.shape, F32),
            pltpu.VMEM(border.shape, F32),
            pltpu.SemaphoreType.DMA(()),
            pltpu.SemaphoreType.DMA((4, len(STATE_BLOCKS))),
            pltpu.SemaphoreType.DMA((3, len(STATE_BLOCKS))),
            pltpu.VMEM((SUBS * PITCH, LANES), F32),
            pltpu.VMEM((SUBS * PITCH, LANES), F32),
            square,
            pltpu.VMEM((tokens // SUBS, LANES), F32),
            tile,
            tile,
        ],
        compiler_params=pltpu.CompilerParams(vmem_limit_bytes=STATES_VMEM),
        cost_estimate=work(tokens, channels, 96, 16),
        name="states",
    )(*signals, rates)


def outputs_call(signals, rates, conv, grad, entries):
    tokens, channels = signals[0].shape
    signal_type = signals[0].dtype
    signal_buffer = pltpu.VMEM((tokens, channels), signal_type)
    here = pl.BlockSpec(memory_space=pltpu.VMEM)
    there = pl.BlockSpec(memory_space=pltpu.HBM)
    result = jax.ShapeDtypeStruct((tokens, channels), signal_type)
    return pl.pallas_call(
        output_kernel,
        in_specs=[here] * 5 + [there] * 2 + [here],
        out_specs=[there] * 4,
        out_shape=[result] * 4,
        scratch_shapes=[pltpu.VMEM((tokens, channels), F32)] * 2
        + [signal_buffer] * 4
        + [pltpu.SemaphoreType.DMA((2, OUTPUT_COLUMNS)), pltpu.SemaphoreType.DMA((4, OUTPUT_COLUMNS))]
        + [pltpu.VMEM((tokens, channels), F32)] * 2,
        compiler_params=pltpu.CompilerParams(vmem_limit_bytes=OUTPUTS_VMEM),
        cost_estimate=work(tokens, channels, 64, 24),
        name="outputs",
    )(*signals, rates, conv, grad, entries)


def on_device(query_input, key_input, value_input, cotangent, residues, decay_rates):
    tokens, channels = query_input.shape[1:]
    modes = residues.shape[1]
    ctx_count = lax.axis_size("ctx")
    seq_count = lax.axis_size("seq")
    blocks = channels // LANES
    halves = modes // MODES_TILE
    signals = [s[0] for s in (query_input, key_input, value_input, cotangent)]
    rates = decay_rates.T
    modal = residues.T

    here = pl.BlockSpec(memory_space=pltpu.VMEM)
    whole = jax.ShapeDtypeStruct((tokens, channels), F32)
    square = pltpu.VMEM((tokens, LANES), F32)
    small = pltpu.CompilerParams(vmem_limit_bytes=SMALL_VMEM)

    packed, before, after = states_call(signals, rates)

    gathered = lax.all_to_all(
        packed.reshape(ctx_count, 3 * MODES_TILE, LANES), "ctx", split_axis=0, concat_axis=0, tiled=True
    )

    per_step = blocks // GROUPS
    signal_spec = pl.BlockSpec((tokens, per_step * LANES), lambda i: (0, i))
    mode_spec = pl.BlockSpec((modes, per_step * LANES), lambda i: (0, i))
    border_spec = pl.BlockSpec((per_step, halves, MODES_TILE * SUBS, LANES), lambda i: (i, 0, 0, 0))
    conv, grad = pl.pallas_call(
        local_kernel,
        grid=(GROUPS,),
        in_specs=[signal_spec] * 4 + [mode_spec] * 2 + [border_spec] * 2,
        out_specs=[signal_spec] * 2,
        out_shape=[whole] * 2,
        scratch_shapes=[square] * 4,
        cost_estimate=work(tokens, channels, 128, 24),
        name="local",
    )(*signals, rates, modal, before, after)
    gathered, conv, grad = lax.optimization_barrier((gathered, conv, grad))

    borders, part = pl.pallas_call(
        functools.partial(scan_kernel, tokens, blocks, 1.0 / (tokens * ctx_count * seq_count)),
        in_specs=[here] * 3,
        out_specs=[here] * 2,
        out_shape=[
            jax.ShapeDtypeStruct((ctx_count, 2 * MODES_TILE, LANES), F32),
            jax.ShapeDtypeStruct((MODES_TILE, LANES), F32),
        ],
        compiler_params=small,
        name="scan",
    )(gathered, rates, modal)

    near, far, cross = (
        lax.ppermute(part, "seq", [(i, i ^ flip) for i in range(seq_count)]) for flip in (1, 2, 3)
    )
    part = (part + near) + (far + cross)
    repacked = pl.pallas_call(
        pack_kernel,
        in_specs=[here] * 2,
        out_specs=here,
        out_shape=jax.ShapeDtypeStruct((ctx_count, 3 * MODES_TILE, LANES), F32),
        compiler_params=small,
        name="pack",
    )(borders, part)
    returned = lax.all_to_all(repacked, "ctx", split_axis=0, concat_axis=0, tiled=True)

    entries = returned.reshape(halves, blocks, 3 * MODES_TILE, LANES)
    results = outputs_call(signals, rates, conv, grad, entries)
    tiles = returned[:, 2 * MODES_TILE :]
    tiles = tiles + lax.ppermute(tiles, "seq", [(i, i ^ 6) for i in range(seq_count)])
    grad_rows = tiles.reshape(halves, blocks, MODES_TILE, LANES).transpose(0, 2, 1, 3)
    return (*[r[None] for r in results], grad_rows.reshape(modes, channels).T)


def solution(mesh):
    split = P("seq", "ctx", None)
    return jax.shard_map(
        on_device,
        mesh=mesh,
        in_specs=(split, split, split, split, P(), P()),
        out_specs=(split, split, split, split, P()),
        check_vma=False,
    )
```

```python
import functools

import jax
import jax.numpy as jnp
from jax import lax
from jax.experimental import pallas as pl
from jax.experimental.pallas import tpu as pltpu
from jax.sharding import PartitionSpec as P

LANES = 128
SUBS = 8
SPARE = 8
MODES_TILE = 8
F32 = jnp.float32
GROUPS = 4
OUTPUT_COLUMNS = 2
STATE_BLOCKS = (4, 4, 4, 4)
AHEAD = 2
UNROLL = 4
PITCH = 17
SMALL_VMEM = 12 * 1024 * 1024
STATES_VMEM = 58 * 1024 * 1024
OUTPUTS_VMEM = 51 * 1024 * 1024


def sub_index():
    return lax.broadcasted_iota(jnp.int32, (SUBS, LANES), 0)


def scale_of(rates):
    bent = jnp.tanh(rates)
    return jnp.sqrt(2.0 * bent / (1.0 + bent))


def rows_of(tile):
    return [jnp.broadcast_to(tile[m : m + 1], (SUBS, LANES)) for m in range(MODES_TILE)]


def states_kernel(
    query_hbm,
    key_hbm,
    value_hbm,
    cot_hbm,
    rates_hbm,
    packed_hbm,
    before_hbm,
    after_hbm,
    query_ref,
    key_ref,
    value_ref,
    cot_ref,
    rates_ref,
    packed_ref,
    before_ref,
    after_ref,
    rates_arrived,
    arrived,
    sent,
    u_ref,
    a_ref,
    lag_ref,
    lag_sum_ref,
    fwd_ref,
    bwd_ref,
):
    tokens, width = query_ref.shape
    steps = tokens // SUBS
    modes = rates_ref.shape[0]
    firsts = [sum(STATE_BLOCKS[:n]) for n in range(len(STATE_BLOCKS))]
    pairs = ((query_hbm, query_ref), (key_hbm, key_ref), (value_hbm, value_ref), (cot_hbm, cot_ref))

    def fetches(group):
        lanes = pl.ds(firsts[group] * LANES, STATE_BLOCKS[group] * LANES)
        return [
            pltpu.make_async_copy(source.at[:, lanes], target.at[:, lanes], arrived.at[n, group])
            for n, (source, target) in enumerate(pairs)
        ]

    def stores(group):
        part = pl.ds(firsts[group], STATE_BLOCKS[group])
        rows = pl.ds(0, MODES_TILE * SUBS)
        return [
            pltpu.make_async_copy(packed_ref.at[:, part], packed_hbm.at[:, part], sent.at[0, group]),
            pltpu.make_async_copy(before_ref.at[part, :, rows], before_hbm.at[part], sent.at[1, group]),
            pltpu.make_async_copy(after_ref.at[part, :, rows], after_hbm.at[part], sent.at[2, group]),
        ]

    rates_fetch = pltpu.make_async_copy(rates_hbm, rates_ref, rates_arrived)
    rates_fetch.start()
    for group in range(AHEAD):
        for fetch in fetches(group):
            fetch.start()
    rates_fetch.wait()

    def block(index, carry):
        lanes = pl.ds(pl.multiple_of(index * LANES, LANES), LANES)
        mixed = key_ref[:, lanes].astype(F32) * value_ref[:, lanes].astype(F32)
        adjoint = cot_ref[:, lanes].astype(F32) * query_ref[:, lanes].astype(F32)
        for s in range(SUBS):
            u_ref[s * PITCH : s * PITCH + steps, :] = mixed[s * steps : (s + 1) * steps]
            a_ref[s * PITCH : s * PITCH + steps, :] = adjoint[s * steps : (s + 1) * steps]
        u = [u_ref[pl.ds(i, SUBS, stride=PITCH), :] for i in range(steps)]
        a = [a_ref[pl.ds(i, SUBS, stride=PITCH), :] for i in range(steps)]
        for lag in range(steps):
            total = a[lag] * u[0]
            for i in range(1, steps - lag):
                total = total + a[lag + i] * u[i]
            lag_ref[lag * SUBS : (lag + 1) * SUBS, :] = total
        for group in range(steps // SUBS):
            total = None
            for s in range(SUBS):
                term = lag_ref[pl.ds(group * SUBS * SUBS + s, SUBS, stride=SUBS), :]
                total = term if total is None else total + term
            lag_sum_ref[group * SUBS : (group + 1) * SUBS, :] = total
        for half in range(modes // MODES_TILE):
            rates = rates_ref[half * MODES_TILE : (half + 1) * MODES_TILE, lanes]
            lam_tile = jnp.exp(-rates)
            lam = rows_of(lam_tile)
            fwd = [u_ref[pl.ds(0, SUBS, stride=PITCH), :]] * MODES_TILE
            bwd = [a_ref[pl.ds(steps - 1, SUBS, stride=PITCH), :]] * MODES_TILE
            for i in range(1, steps):
                front = u_ref[pl.ds(i, SUBS, stride=PITCH), :]
                back = a_ref[pl.ds(steps - 1 - i, SUBS, stride=PITCH), :]
                for m in range(MODES_TILE):
                    fwd[m] = lam[m] * fwd[m] + front
                    bwd[m] = lam[m] * bwd[m] + back
            for m in range(MODES_TILE):
                fwd_ref[m * SUBS : (m + 1) * SUBS, :] = fwd[m]
                bwd_ref[m * SUBS : (m + 1) * SUBS, :] = bwd[m]
            jump = jnp.exp(rates * -float(steps))
            zero = jnp.zeros((MODES_TILE, LANES), F32)
            before, after, cross, inner = zero, zero, zero, zero
            for s in range(SUBS):
                rows = pl.ds(s, MODES_TILE, stride=SUBS)
                before_ref[index, half, rows, :] = before
                cross = cross + bwd_ref[rows, :] * before
                before = jump * before + fwd_ref[rows, :]
            for s in reversed(range(SUBS)):
                rows = pl.ds(s, MODES_TILE, stride=SUBS)
                after_ref[index, half, rows, :] = after
                after = jump * after + bwd_ref[rows, :]
            for lag in reversed(range(steps)):
                inner = inner * lam_tile + lag_sum_ref[lag : lag + 1, :]
            packed_ref[half, index, 0:MODES_TILE, :] = before
            packed_ref[half, index, MODES_TILE : 2 * MODES_TILE, :] = after
            packed_ref[half, index, 2 * MODES_TILE : 3 * MODES_TILE, :] = inner + lam_tile * cross
        return carry

    for group, (first, count) in enumerate(zip(firsts, STATE_BLOCKS, strict=True)):
        for fetch in fetches(group):
            fetch.wait()
        if group + AHEAD < len(firsts):
            for fetch in fetches(group + AHEAD):
                fetch.start()
        if UNROLL >= count:
            for index in range(first, first + count):
                block(index, 0)
        else:
            lax.fori_loop(first, first + count, block, 0, unroll=UNROLL)
        for store in stores(group):
            store.start()
    for group in range(len(firsts)):
        for store in stores(group):
            store.wait()


def local_kernel(
    query_ref,
    key_ref,
    value_ref,
    cot_ref,
    rates_ref,
    residues_ref,
    before_ref,
    after_ref,
    conv_ref,
    grad_ref,
    u_ref,
    a_ref,
    y_ref,
    g_ref,
):
    tokens, width = query_ref.shape
    steps = tokens // SUBS
    modes = rates_ref.shape[0]

    def block(index, carry):
        lanes = pl.ds(pl.multiple_of(index * LANES, LANES), LANES)
        u_ref[0:tokens] = key_ref[:, lanes].astype(F32) * value_ref[:, lanes].astype(F32)
        a_ref[0:tokens] = cot_ref[:, lanes].astype(F32) * query_ref[:, lanes].astype(F32)
        for half in range(modes // MODES_TILE):
            picked = slice(half * MODES_TILE, (half + 1) * MODES_TILE)
            rates = rates_ref[picked, lanes]
            lam = rows_of(jnp.exp(-rates))
            weight = rows_of(residues_ref[picked, lanes] * scale_of(rates))
            fwd = [before_ref[index, half, m * SUBS : (m + 1) * SUBS, :] for m in range(MODES_TILE)]
            for i in range(steps):
                rows = pl.ds(i, SUBS, stride=steps)
                u = u_ref[rows, :]
                total = y_ref[rows, :] if half else None
                for m in range(MODES_TILE):
                    fwd[m] = lam[m] * fwd[m] + u
                    term = weight[m] * fwd[m]
                    total = term if total is None else total + term
                y_ref[rows, :] = total
            bwd = [after_ref[index, half, m * SUBS : (m + 1) * SUBS, :] for m in range(MODES_TILE)]
            for i in reversed(range(steps)):
                rows = pl.ds(i, SUBS, stride=steps)
                a = a_ref[rows, :]
                total = g_ref[rows, :] if half else None
                for m in range(MODES_TILE):
                    bwd[m] = lam[m] * bwd[m] + a
                    term = weight[m] * bwd[m]
                    total = term if total is None else total + term
                g_ref[rows, :] = total
        conv_ref[:, lanes] = y_ref[0:tokens]
        grad_ref[:, lanes] = g_ref[0:tokens]
        return carry

    lax.fori_loop(0, width // LANES, block, 0)


def scan_kernel(chunk_tokens, per_half, share, states_ref, rates_ref, residues_ref, out_ref, part_ref):
    chunks = states_ref.shape[0]
    rank = lax.axis_index("ctx")
    rows = pl.ds(pl.multiple_of((rank // per_half) * MODES_TILE, MODES_TILE), MODES_TILE)
    lanes = pl.ds(pl.multiple_of((rank % per_half) * LANES, LANES), LANES)
    rates = rates_ref[rows, lanes]
    lam = jnp.exp(-rates)
    jump = jnp.exp(rates * -float(chunk_tokens))
    scaling = scale_of(rates)
    entry = residues_ref[rows, lanes] * scaling * lam
    zero = jnp.zeros((MODES_TILE, LANES), F32)
    fwd, cross, inner = zero, zero, zero
    for j in range(chunks):
        out_ref[j, 0:MODES_TILE] = entry * fwd
        cross = cross + states_ref[j, MODES_TILE : 2 * MODES_TILE] * fwd
        inner = inner + states_ref[j, 2 * MODES_TILE : 3 * MODES_TILE]
        fwd = jump * fwd + states_ref[j, 0:MODES_TILE]
    bwd = zero
    for j in reversed(range(chunks)):
        out_ref[j, MODES_TILE : 2 * MODES_TILE] = entry * bwd
        bwd = jump * bwd + states_ref[j, MODES_TILE : 2 * MODES_TILE]
    part = (inner + lam * cross) * scaling * share
    part_ref[...] = part


def pack_kernel(states_ref, part_ref, out_ref):
    for j in range(out_ref.shape[0]):
        out_ref[j, 0 : 2 * MODES_TILE] = states_ref[j]
        out_ref[j, 2 * MODES_TILE : 3 * MODES_TILE] = part_ref[...]


def output_kernel(
    query_ref,
    key_ref,
    value_ref,
    cot_ref,
    rates_ref,
    conv_hbm,
    grad_hbm,
    entry_ref,
    out_hbm,
    grad_query_hbm,
    grad_key_hbm,
    grad_value_hbm,
    conv_ref,
    grad_ref,
    out_ref,
    grad_query_ref,
    grad_key_ref,
    grad_value_ref,
    arrived,
    sent,
    y_ref,
    g_ref,
):
    tokens, width = query_ref.shape
    modes = rates_ref.shape[0]
    groups = tokens // SUBS
    sub = sub_index().astype(F32)
    columns = sent.shape[1]
    span = width // columns
    pairs = (
        (out_ref, out_hbm),
        (grad_query_ref, grad_query_hbm),
        (grad_key_ref, grad_key_hbm),
        (grad_value_ref, grad_value_hbm),
    )

    inputs = (
        (conv_hbm, conv_ref),
        (grad_hbm, grad_ref),
    )

    def fetches(column):
        lanes = pl.ds(column * span, span)
        return [
            pltpu.make_async_copy(source.at[:, lanes], target.at[:, lanes], arrived.at[n, column])
            for n, (source, target) in enumerate(inputs)
        ]

    for column in range(columns):
        for fetch in fetches(column):
            fetch.start()

    def stores(column):
        lanes = pl.ds(column * span, span)
        return [
            pltpu.make_async_copy(source.at[:, lanes], target.at[:, lanes], sent.at[n, column])
            for n, (source, target) in enumerate(pairs)
        ]

    def entry(index, carry):
        lanes = pl.ds(pl.multiple_of(index * LANES, LANES), LANES)
        for half in range(modes // MODES_TILE):
            picked = slice(half * MODES_TILE, (half + 1) * MODES_TILE)
            rates = rates_ref[picked, lanes]
            row = rows_of(rates)
            jump = rows_of(jnp.exp(rates * -float(SUBS)))
            early = rows_of(entry_ref[half, index, 0:MODES_TILE, :])
            late = rows_of(entry_ref[half, index, MODES_TILE : 2 * MODES_TILE, :])
            fwd = [early[m] * jnp.exp(-row[m] * sub) for m in range(MODES_TILE)]
            bwd = [late[m] * jnp.exp(-row[m] * (SUBS - 1 - sub)) for m in range(MODES_TILE)]
            for i in range(groups):
                rows = slice(i * SUBS, (i + 1) * SUBS)
                total = y_ref[rows, lanes] if half else None
                for m in range(MODES_TILE):
                    total = fwd[m] if total is None else total + fwd[m]
                    fwd[m] = fwd[m] * jump[m]
                y_ref[rows, lanes] = total
                rows = slice((groups - 1 - i) * SUBS, (groups - i) * SUBS)
                total = g_ref[rows, lanes] if half else None
                for m in range(MODES_TILE):
                    total = bwd[m] if total is None else total + bwd[m]
                    bwd[m] = bwd[m] * jump[m]
                g_ref[rows, lanes] = total
        return carry

    def finish(index, carry):
        lanes = pl.ds(pl.multiple_of(index * LANES, LANES), LANES)
        y = y_ref[:, lanes] + conv_ref[:, lanes]
        g = g_ref[:, lanes] + grad_ref[:, lanes]
        out_ref[:, lanes] = (query_ref[:, lanes].astype(F32) * y).astype(out_ref.dtype)
        grad_query_ref[:, lanes] = (cot_ref[:, lanes].astype(F32) * y).astype(out_ref.dtype)
        grad_key_ref[:, lanes] = (value_ref[:, lanes].astype(F32) * g).astype(out_ref.dtype)
        grad_value_ref[:, lanes] = (key_ref[:, lanes].astype(F32) * g).astype(out_ref.dtype)
        return carry

    count = span // LANES
    for column in range(columns):
        first = column * count
        lax.fori_loop(first, first + count, entry, 0, unroll=True)
        for fetch in fetches(column):
            fetch.wait()
        lax.fori_loop(first, first + count, finish, 0, unroll=True)
        for store in stores(column):
            store.start()
    for column in range(columns):
        for store in stores(column):
            store.wait()


def work(tokens, channels, ops, moved):
    return pl.CostEstimate(
        flops=ops * tokens * channels, bytes_accessed=moved * tokens * channels, transcendentals=0
    )


def states_call(signals, rates):
    tokens, channels = signals[0].shape
    modes = rates.shape[0]
    blocks = channels // LANES
    halves = modes // MODES_TILE
    there = pl.BlockSpec(memory_space=pltpu.HBM)
    border = jax.ShapeDtypeStruct((blocks, halves, MODES_TILE * SUBS, LANES), F32)
    square = pltpu.VMEM((tokens + SPARE, LANES), F32)
    tile = pltpu.VMEM((MODES_TILE * SUBS + SPARE, LANES), F32)
    staged = pltpu.VMEM((blocks, halves, MODES_TILE * SUBS + SPARE, LANES), F32)
    signal_buffer = pltpu.VMEM((tokens, channels), signals[0].dtype)
    return pl.pallas_call(
        states_kernel,
        in_specs=[there] * 5,
        out_specs=[there] * 3,
        out_shape=[jax.ShapeDtypeStruct((halves, blocks, 3 * MODES_TILE, LANES), F32), border, border],
        scratch_shapes=[signal_buffer] * 4
        + [
            pltpu.VMEM((modes, channels), F32),
            pltpu.VMEM((halves, blocks, 3 * MODES_TILE, LANES), F32),
            staged,
            staged,
            pltpu.SemaphoreType.DMA(()),
            pltpu.SemaphoreType.DMA((4, len(STATE_BLOCKS))),
            pltpu.SemaphoreType.DMA((3, len(STATE_BLOCKS))),
            pltpu.VMEM((SUBS * PITCH + 2 * SPARE, LANES), F32),
            pltpu.VMEM((SUBS * PITCH + 2 * SPARE, LANES), F32),
            square,
            pltpu.VMEM((tokens // SUBS, LANES), F32),
            tile,
            tile,
        ],
        compiler_params=pltpu.CompilerParams(vmem_limit_bytes=STATES_VMEM),
        cost_estimate=work(tokens, channels, 96, 16),
        name="states",
    )(*signals, rates)


def outputs_call(signals, rates, conv, grad, entries):
    tokens, channels = signals[0].shape
    signal_type = signals[0].dtype
    signal_buffer = pltpu.VMEM((tokens, channels), signal_type)
    here = pl.BlockSpec(memory_space=pltpu.VMEM)
    there = pl.BlockSpec(memory_space=pltpu.HBM)
    result = jax.ShapeDtypeStruct((tokens, channels), signal_type)
    return pl.pallas_call(
        output_kernel,
        in_specs=[here] * 5 + [there] * 2 + [here],
        out_specs=[there] * 4,
        out_shape=[result] * 4,
        scratch_shapes=[pltpu.VMEM((tokens, channels), F32)] * 2
        + [signal_buffer] * 4
        + [pltpu.SemaphoreType.DMA((2, OUTPUT_COLUMNS)), pltpu.SemaphoreType.DMA((4, OUTPUT_COLUMNS))]
        + [pltpu.VMEM((tokens, channels), F32)] * 2,
        compiler_params=pltpu.CompilerParams(vmem_limit_bytes=OUTPUTS_VMEM),
        cost_estimate=work(tokens, channels, 64, 24),
        name="outputs",
    )(*signals, rates, conv, grad, entries)


def on_device(query_input, key_input, value_input, cotangent, residues, decay_rates):
    tokens, channels = query_input.shape[1:]
    modes = residues.shape[1]
    ctx_count = lax.axis_size("ctx")
    seq_count = lax.axis_size("seq")
    blocks = channels // LANES
    halves = modes // MODES_TILE
    signals = [s[0] for s in (query_input, key_input, value_input, cotangent)]
    rates = decay_rates.T
    modal = residues.T

    here = pl.BlockSpec(memory_space=pltpu.VMEM)
    whole = jax.ShapeDtypeStruct((tokens, channels), F32)
    square = pltpu.VMEM((tokens + 2 * SPARE, LANES), F32)
    small = pltpu.CompilerParams(vmem_limit_bytes=SMALL_VMEM)

    packed, before, after = states_call(signals, rates)

    gathered = lax.all_to_all(
        packed.reshape(ctx_count, 3 * MODES_TILE, LANES), "ctx", split_axis=0, concat_axis=0, tiled=True
    )

    per_step = blocks // GROUPS
    signal_spec = pl.BlockSpec((tokens, per_step * LANES), lambda i: (0, i))
    mode_spec = pl.BlockSpec((modes, per_step * LANES), lambda i: (0, i))
    border_spec = pl.BlockSpec((per_step, halves, MODES_TILE * SUBS, LANES), lambda i: (i, 0, 0, 0))
    conv, grad = pl.pallas_call(
        local_kernel,
        grid=(GROUPS,),
        in_specs=[signal_spec] * 4 + [mode_spec] * 2 + [border_spec] * 2,
        out_specs=[signal_spec] * 2,
        out_shape=[whole] * 2,
        scratch_shapes=[square] * 4,
        cost_estimate=work(tokens, channels, 128, 24),
        name="local",
    )(*signals, rates, modal, before, after)
    gathered, conv, grad = lax.optimization_barrier((gathered, conv, grad))

    borders, part = pl.pallas_call(
        functools.partial(scan_kernel, tokens, blocks, 1.0 / (tokens * ctx_count * seq_count)),
        in_specs=[here] * 3,
        out_specs=[here] * 2,
        out_shape=[
            jax.ShapeDtypeStruct((ctx_count, 2 * MODES_TILE, LANES), F32),
            jax.ShapeDtypeStruct((MODES_TILE, LANES), F32),
        ],
        compiler_params=small,
        name="scan",
    )(gathered, rates, modal)

    near, far, cross = (
        lax.ppermute(part, "seq", [(i, i ^ flip) for i in range(seq_count)]) for flip in (1, 2, 3)
    )
    part = (part + near) + (far + cross)
    repacked = pl.pallas_call(
        pack_kernel,
        in_specs=[here] * 2,
        out_specs=here,
        out_shape=jax.ShapeDtypeStruct((ctx_count, 3 * MODES_TILE, LANES), F32),
        compiler_params=small,
        name="pack",
    )(borders, part)
    returned = lax.all_to_all(repacked, "ctx", split_axis=0, concat_axis=0, tiled=True)

    entries = returned.reshape(halves, blocks, 3 * MODES_TILE, LANES)
    results = outputs_call(signals, rates, conv, grad, entries)
    tiles = returned[:, 2 * MODES_TILE :]
    tiles = tiles + lax.ppermute(tiles, "seq", [(i, i ^ 6) for i in range(seq_count)])
    grad_rows = tiles.reshape(halves, blocks, MODES_TILE, LANES).transpose(0, 2, 1, 3)
    return (*[r[None] for r in results], grad_rows.reshape(modes, channels).T)


def solution(mesh):
    split = P("seq", "ctx", None)
    return jax.shard_map(
        on_device,
        mesh=mesh,
        in_specs=(split, split, split, split, P(), P()),
        out_specs=(split, split, split, split, P()),
        check_vma=False,
    )
```

```python
import functools

import jax
import jax.numpy as jnp
from jax import lax
from jax.experimental import pallas as pl
from jax.experimental.pallas import tpu as pltpu
from jax.sharding import PartitionSpec as P

LANES = 128
SUBS = 8
SPARE = 8
MODES_TILE = 8
F32 = jnp.float32
GROUPS = 4
OUTPUT_COLUMNS = 2
STATE_BLOCKS = (4, 4, 4, 4)
AHEAD = 2
UNROLL = 4
PITCH = 17
SMALL_VMEM = 12 * 1024 * 1024
STATES_VMEM = 58 * 1024 * 1024
OUTPUTS_VMEM = 51 * 1024 * 1024


def sub_index():
    return lax.broadcasted_iota(jnp.int32, (SUBS, LANES), 0)


def scale_of(rates):
    bent = jnp.tanh(rates)
    return jnp.sqrt(2.0 * bent / (1.0 + bent))


def rows_of(tile):
    return [jnp.broadcast_to(tile[m : m + 1], (SUBS, LANES)) for m in range(MODES_TILE)]


def states_kernel(
    query_hbm,
    key_hbm,
    value_hbm,
    cot_hbm,
    rates_hbm,
    packed_hbm,
    before_hbm,
    after_hbm,
    query_ref,
    key_ref,
    value_ref,
    cot_ref,
    rates_ref,
    packed_ref,
    before_ref,
    after_ref,
    rates_arrived,
    arrived,
    sent,
    u_ref,
    a_ref,
    lag_ref,
    lag_sum_ref,
    fwd_ref,
    bwd_ref,
    mid_ref,
):
    tokens, width = query_ref.shape
    steps = tokens // SUBS
    modes = rates_ref.shape[0]
    firsts = [sum(STATE_BLOCKS[:n]) for n in range(len(STATE_BLOCKS))]
    pairs = ((query_hbm, query_ref), (key_hbm, key_ref), (value_hbm, value_ref), (cot_hbm, cot_ref))

    def fetches(group):
        lanes = pl.ds(firsts[group] * LANES, STATE_BLOCKS[group] * LANES)
        return [
            pltpu.make_async_copy(source.at[:, lanes], target.at[:, lanes], arrived.at[n, group])
            for n, (source, target) in enumerate(pairs)
        ]

    def stores(group):
        part = pl.ds(firsts[group], STATE_BLOCKS[group])
        rows = pl.ds(0, MODES_TILE * SUBS)
        return [
            pltpu.make_async_copy(packed_ref.at[:, part], packed_hbm.at[:, part], sent.at[0, group]),
            pltpu.make_async_copy(before_ref.at[part, :, rows], before_hbm.at[part], sent.at[1, group]),
            pltpu.make_async_copy(after_ref.at[part, :, rows], after_hbm.at[part], sent.at[2, group]),
        ]

    rates_fetch = pltpu.make_async_copy(rates_hbm, rates_ref, rates_arrived)
    rates_fetch.start()
    for group in range(AHEAD):
        for fetch in fetches(group):
            fetch.start()
    rates_fetch.wait()

    def block(index, carry):
        lanes = pl.ds(pl.multiple_of(index * LANES, LANES), LANES)
        mixed = key_ref[:, lanes].astype(F32) * value_ref[:, lanes].astype(F32)
        adjoint = cot_ref[:, lanes].astype(F32) * query_ref[:, lanes].astype(F32)
        for s in range(SUBS):
            u_ref[s * PITCH : s * PITCH + steps, :] = mixed[s * steps : (s + 1) * steps]
            a_ref[s * PITCH : s * PITCH + steps, :] = adjoint[s * steps : (s + 1) * steps]
        u = [u_ref[pl.ds(i, SUBS, stride=PITCH), :] for i in range(steps)]
        a = [a_ref[pl.ds(i, SUBS, stride=PITCH), :] for i in range(steps)]
        middle = steps // 2
        for lag in range(middle):
            total = None
            for start in (0, middle):
                for i in range(start, start + middle - lag):
                    term = a[lag + i] * u[i]
                    total = term if total is None else total + term
            lag_ref[lag * SUBS : (lag + 1) * SUBS, :] = total
        total = None
        for s in range(SUBS):
            term = lag_ref[pl.ds(s, middle, stride=SUBS), :]
            total = term if total is None else total + term
        lag_sum_ref[...] = total
        for half in range(modes // MODES_TILE):
            rates = rates_ref[half * MODES_TILE : (half + 1) * MODES_TILE, lanes]
            lam_tile = jnp.exp(-rates)
            lam = rows_of(lam_tile)
            fwd = [u_ref[pl.ds(0, SUBS, stride=PITCH), :]] * MODES_TILE
            bwd = [a_ref[pl.ds(steps - 1, SUBS, stride=PITCH), :]] * MODES_TILE
            for i in range(1, steps):
                front = u_ref[pl.ds(i, SUBS, stride=PITCH), :]
                back = a_ref[pl.ds(steps - 1 - i, SUBS, stride=PITCH), :]
                for m in range(MODES_TILE):
                    fwd[m] = lam[m] * fwd[m] + front
                    bwd[m] = lam[m] * bwd[m] + back
                if i == middle - 1:
                    for m in range(MODES_TILE):
                        mid_ref[m * SUBS : (m + 1) * SUBS, :] = fwd[m] * bwd[m]
            for m in range(MODES_TILE):
                fwd_ref[m * SUBS : (m + 1) * SUBS, :] = fwd[m]
                bwd_ref[m * SUBS : (m + 1) * SUBS, :] = bwd[m]
            jump = jnp.exp(rates * -float(steps))
            zero = jnp.zeros((MODES_TILE, LANES), F32)
            before, after, cross, inner = zero, zero, zero, zero
            for s in range(SUBS):
                rows = pl.ds(s, MODES_TILE, stride=SUBS)
                before_ref[index, half, rows, :] = before
                cross = cross + bwd_ref[rows, :] * before + mid_ref[rows, :]
                before = jump * before + fwd_ref[rows, :]
            for s in reversed(range(SUBS)):
                rows = pl.ds(s, MODES_TILE, stride=SUBS)
                after_ref[index, half, rows, :] = after
                after = jump * after + bwd_ref[rows, :]
            for lag in reversed(range(middle)):
                inner = inner * lam_tile + lag_sum_ref[lag : lag + 1, :]
            packed_ref[half, index, 0:MODES_TILE, :] = before
            packed_ref[half, index, MODES_TILE : 2 * MODES_TILE, :] = after
            packed_ref[half, index, 2 * MODES_TILE : 3 * MODES_TILE, :] = inner + lam_tile * cross
        return carry

    for group, (first, count) in enumerate(zip(firsts, STATE_BLOCKS, strict=True)):
        for fetch in fetches(group):
            fetch.wait()
        if group + AHEAD < len(firsts):
            for fetch in fetches(group + AHEAD):
                fetch.start()
        if UNROLL >= count:
            for index in range(first, first + count):
                block(index, 0)
        else:
            lax.fori_loop(first, first + count, block, 0, unroll=UNROLL)
        for store in stores(group):
            store.start()
    for group in range(len(firsts)):
        for store in stores(group):
            store.wait()


def local_kernel(
    query_ref,
    key_ref,
    value_ref,
    cot_ref,
    rates_ref,
    residues_ref,
    before_ref,
    after_ref,
    conv_ref,
    grad_ref,
    u_ref,
    a_ref,
    y_ref,
    g_ref,
):
    tokens, width = query_ref.shape
    steps = tokens // SUBS
    modes = rates_ref.shape[0]

    def block(index, carry):
        lanes = pl.ds(pl.multiple_of(index * LANES, LANES), LANES)
        u_ref[0:tokens] = key_ref[:, lanes].astype(F32) * value_ref[:, lanes].astype(F32)
        a_ref[0:tokens] = cot_ref[:, lanes].astype(F32) * query_ref[:, lanes].astype(F32)
        for half in range(modes // MODES_TILE):
            picked = slice(half * MODES_TILE, (half + 1) * MODES_TILE)
            rates = rates_ref[picked, lanes]
            lam = rows_of(jnp.exp(-rates))
            weight = rows_of(residues_ref[picked, lanes] * scale_of(rates))
            fwd = [before_ref[index, half, m * SUBS : (m + 1) * SUBS, :] for m in range(MODES_TILE)]
            for i in range(steps):
                rows = pl.ds(i, SUBS, stride=steps)
                u = u_ref[rows, :]
                total = y_ref[rows, :] if half else None
                for m in range(MODES_TILE):
                    fwd[m] = lam[m] * fwd[m] + u
                    term = weight[m] * fwd[m]
                    total = term if total is None else total + term
                y_ref[rows, :] = total
            bwd = [after_ref[index, half, m * SUBS : (m + 1) * SUBS, :] for m in range(MODES_TILE)]
            for i in reversed(range(steps)):
                rows = pl.ds(i, SUBS, stride=steps)
                a = a_ref[rows, :]
                total = g_ref[rows, :] if half else None
                for m in range(MODES_TILE):
                    bwd[m] = lam[m] * bwd[m] + a
                    term = weight[m] * bwd[m]
                    total = term if total is None else total + term
                g_ref[rows, :] = total
        conv_ref[:, lanes] = y_ref[0:tokens]
        grad_ref[:, lanes] = g_ref[0:tokens]
        return carry

    lax.fori_loop(0, width // LANES, block, 0)


def scan_kernel(chunk_tokens, per_half, share, states_ref, rates_ref, residues_ref, out_ref, part_ref):
    chunks = states_ref.shape[0]
    rank = lax.axis_index("ctx")
    rows = pl.ds(pl.multiple_of((rank // per_half) * MODES_TILE, MODES_TILE), MODES_TILE)
    lanes = pl.ds(pl.multiple_of((rank % per_half) * LANES, LANES), LANES)
    rates = rates_ref[rows, lanes]
    lam = jnp.exp(-rates)
    jump = jnp.exp(rates * -float(chunk_tokens))
    scaling = scale_of(rates)
    entry = residues_ref[rows, lanes] * scaling * lam
    zero = jnp.zeros((MODES_TILE, LANES), F32)
    fwd, cross, inner = zero, zero, zero
    for j in range(chunks):
        out_ref[j, 0:MODES_TILE] = entry * fwd
        cross = cross + states_ref[j, MODES_TILE : 2 * MODES_TILE] * fwd
        inner = inner + states_ref[j, 2 * MODES_TILE : 3 * MODES_TILE]
        fwd = jump * fwd + states_ref[j, 0:MODES_TILE]
    bwd = zero
    for j in reversed(range(chunks)):
        out_ref[j, MODES_TILE : 2 * MODES_TILE] = entry * bwd
        bwd = jump * bwd + states_ref[j, MODES_TILE : 2 * MODES_TILE]
    part = (inner + lam * cross) * scaling * share
    part_ref[...] = part


def pack_kernel(states_ref, part_ref, out_ref):
    for j in range(out_ref.shape[0]):
        out_ref[j, 0 : 2 * MODES_TILE] = states_ref[j]
        out_ref[j, 2 * MODES_TILE : 3 * MODES_TILE] = part_ref[...]


def output_kernel(
    query_ref,
    key_ref,
    value_ref,
    cot_ref,
    rates_ref,
    conv_hbm,
    grad_hbm,
    entry_ref,
    out_hbm,
    grad_query_hbm,
    grad_key_hbm,
    grad_value_hbm,
    conv_ref,
    grad_ref,
    out_ref,
    grad_query_ref,
    grad_key_ref,
    grad_value_ref,
    arrived,
    sent,
    y_ref,
    g_ref,
):
    tokens, width = query_ref.shape
    modes = rates_ref.shape[0]
    groups = tokens // SUBS
    sub = sub_index().astype(F32)
    columns = sent.shape[1]
    span = width // columns
    pairs = (
        (out_ref, out_hbm),
        (grad_query_ref, grad_query_hbm),
        (grad_key_ref, grad_key_hbm),
        (grad_value_ref, grad_value_hbm),
    )

    inputs = (
        (conv_hbm, conv_ref),
        (grad_hbm, grad_ref),
    )

    def fetches(column):
        lanes = pl.ds(column * span, span)
        return [
            pltpu.make_async_copy(source.at[:, lanes], target.at[:, lanes], arrived.at[n, column])
            for n, (source, target) in enumerate(inputs)
        ]

    for column in range(columns):
        for fetch in fetches(column):
            fetch.start()

    def stores(column):
        lanes = pl.ds(column * span, span)
        return [
            pltpu.make_async_copy(source.at[:, lanes], target.at[:, lanes], sent.at[n, column])
            for n, (source, target) in enumerate(pairs)
        ]

    def entry(index, carry):
        lanes = pl.ds(pl.multiple_of(index * LANES, LANES), LANES)
        for half in range(modes // MODES_TILE):
            picked = slice(half * MODES_TILE, (half + 1) * MODES_TILE)
            rates = rates_ref[picked, lanes]
            row = rows_of(rates)
            jump = rows_of(jnp.exp(rates * -float(SUBS)))
            early = rows_of(entry_ref[half, index, 0:MODES_TILE, :])
            late = rows_of(entry_ref[half, index, MODES_TILE : 2 * MODES_TILE, :])
            fwd = [early[m] * jnp.exp(-row[m] * sub) for m in range(MODES_TILE)]
            bwd = [late[m] * jnp.exp(-row[m] * (SUBS - 1 - sub)) for m in range(MODES_TILE)]
            for i in range(groups):
                rows = slice(i * SUBS, (i + 1) * SUBS)
                total = y_ref[rows, lanes] if half else None
                for m in range(MODES_TILE):
                    total = fwd[m] if total is None else total + fwd[m]
                    fwd[m] = fwd[m] * jump[m]
                y_ref[rows, lanes] = total
                rows = slice((groups - 1 - i) * SUBS, (groups - i) * SUBS)
                total = g_ref[rows, lanes] if half else None
                for m in range(MODES_TILE):
                    total = bwd[m] if total is None else total + bwd[m]
                    bwd[m] = bwd[m] * jump[m]
                g_ref[rows, lanes] = total
        return carry

    def finish(index, carry):
        lanes = pl.ds(pl.multiple_of(index * LANES, LANES), LANES)
        y = y_ref[:, lanes] + conv_ref[:, lanes]
        g = g_ref[:, lanes] + grad_ref[:, lanes]
        out_ref[:, lanes] = (query_ref[:, lanes].astype(F32) * y).astype(out_ref.dtype)
        grad_query_ref[:, lanes] = (cot_ref[:, lanes].astype(F32) * y).astype(out_ref.dtype)
        grad_key_ref[:, lanes] = (value_ref[:, lanes].astype(F32) * g).astype(out_ref.dtype)
        grad_value_ref[:, lanes] = (key_ref[:, lanes].astype(F32) * g).astype(out_ref.dtype)
        return carry

    count = span // LANES
    for column in range(columns):
        first = column * count
        lax.fori_loop(first, first + count, entry, 0, unroll=True)
        for fetch in fetches(column):
            fetch.wait()
        lax.fori_loop(first, first + count, finish, 0, unroll=True)
        for store in stores(column):
            store.start()
    for column in range(columns):
        for store in stores(column):
            store.wait()


def work(tokens, channels, ops, moved):
    return pl.CostEstimate(
        flops=ops * tokens * channels, bytes_accessed=moved * tokens * channels, transcendentals=0
    )


def states_call(signals, rates):
    tokens, channels = signals[0].shape
    modes = rates.shape[0]
    blocks = channels // LANES
    halves = modes // MODES_TILE
    there = pl.BlockSpec(memory_space=pltpu.HBM)
    border = jax.ShapeDtypeStruct((blocks, halves, MODES_TILE * SUBS, LANES), F32)
    tile = pltpu.VMEM((MODES_TILE * SUBS + SPARE, LANES), F32)
    staged = pltpu.VMEM((blocks, halves, MODES_TILE * SUBS + SPARE, LANES), F32)
    signal_buffer = pltpu.VMEM((tokens, channels), signals[0].dtype)
    return pl.pallas_call(
        states_kernel,
        in_specs=[there] * 5,
        out_specs=[there] * 3,
        out_shape=[jax.ShapeDtypeStruct((halves, blocks, 3 * MODES_TILE, LANES), F32), border, border],
        scratch_shapes=[signal_buffer] * 4
        + [
            pltpu.VMEM((modes, channels), F32),
            pltpu.VMEM((halves, blocks, 3 * MODES_TILE, LANES), F32),
            staged,
            staged,
            pltpu.SemaphoreType.DMA(()),
            pltpu.SemaphoreType.DMA((4, len(STATE_BLOCKS))),
            pltpu.SemaphoreType.DMA((3, len(STATE_BLOCKS))),
            pltpu.VMEM((SUBS * PITCH + 2 * SPARE, LANES), F32),
            pltpu.VMEM((SUBS * PITCH + 2 * SPARE, LANES), F32),
            tile,
            pltpu.VMEM((tokens // SUBS // 2, LANES), F32),
            tile,
            tile,
            tile,
        ],
        compiler_params=pltpu.CompilerParams(vmem_limit_bytes=STATES_VMEM),
        cost_estimate=work(tokens, channels, 96, 16),
        name="states",
    )(*signals, rates)


def outputs_call(signals, rates, conv, grad, entries):
    tokens, channels = signals[0].shape
    signal_type = signals[0].dtype
    signal_buffer = pltpu.VMEM((tokens, channels), signal_type)
    here = pl.BlockSpec(memory_space=pltpu.VMEM)
    there = pl.BlockSpec(memory_space=pltpu.HBM)
    result = jax.ShapeDtypeStruct((tokens, channels), signal_type)
    return pl.pallas_call(
        output_kernel,
        in_specs=[here] * 5 + [there] * 2 + [here],
        out_specs=[there] * 4,
        out_shape=[result] * 4,
        scratch_shapes=[pltpu.VMEM((tokens, channels), F32)] * 2
        + [signal_buffer] * 4
        + [pltpu.SemaphoreType.DMA((2, OUTPUT_COLUMNS)), pltpu.SemaphoreType.DMA((4, OUTPUT_COLUMNS))]
        + [pltpu.VMEM((tokens, channels), F32)] * 2,
        compiler_params=pltpu.CompilerParams(vmem_limit_bytes=OUTPUTS_VMEM),
        cost_estimate=work(tokens, channels, 64, 24),
        name="outputs",
    )(*signals, rates, conv, grad, entries)


def on_device(query_input, key_input, value_input, cotangent, residues, decay_rates):
    tokens, channels = query_input.shape[1:]
    modes = residues.shape[1]
    ctx_count = lax.axis_size("ctx")
    seq_count = lax.axis_size("seq")
    blocks = channels // LANES
    halves = modes // MODES_TILE
    signals = [s[0] for s in (query_input, key_input, value_input, cotangent)]
    rates = decay_rates.T
    modal = residues.T

    here = pl.BlockSpec(memory_space=pltpu.VMEM)
    whole = jax.ShapeDtypeStruct((tokens, channels), F32)
    square = pltpu.VMEM((tokens + 2 * SPARE, LANES), F32)
    small = pltpu.CompilerParams(vmem_limit_bytes=SMALL_VMEM)

    packed, before, after = states_call(signals, rates)

    gathered = lax.all_to_all(
        packed.reshape(ctx_count, 3 * MODES_TILE, LANES), "ctx", split_axis=0, concat_axis=0, tiled=True
    )

    per_step = blocks // GROUPS
    signal_spec = pl.BlockSpec((tokens, per_step * LANES), lambda i: (0, i))
    mode_spec = pl.BlockSpec((modes, per_step * LANES), lambda i: (0, i))
    border_spec = pl.BlockSpec((per_step, halves, MODES_TILE * SUBS, LANES), lambda i: (i, 0, 0, 0))
    conv, grad = pl.pallas_call(
        local_kernel,
        grid=(GROUPS,),
        in_specs=[signal_spec] * 4 + [mode_spec] * 2 + [border_spec] * 2,
        out_specs=[signal_spec] * 2,
        out_shape=[whole] * 2,
        scratch_shapes=[square] * 4,
        cost_estimate=work(tokens, channels, 128, 24),
        name="local",
    )(*signals, rates, modal, before, after)
    gathered, conv, grad = lax.optimization_barrier((gathered, conv, grad))

    borders, part = pl.pallas_call(
        functools.partial(scan_kernel, tokens, blocks, 1.0 / (tokens * ctx_count * seq_count)),
        in_specs=[here] * 3,
        out_specs=[here] * 2,
        out_shape=[
            jax.ShapeDtypeStruct((ctx_count, 2 * MODES_TILE, LANES), F32),
            jax.ShapeDtypeStruct((MODES_TILE, LANES), F32),
        ],
        compiler_params=small,
        name="scan",
    )(gathered, rates, modal)

    near, far, cross = (
        lax.ppermute(part, "seq", [(i, i ^ flip) for i in range(seq_count)]) for flip in (1, 2, 3)
    )
    part = (part + near) + (far + cross)
    repacked = pl.pallas_call(
        pack_kernel,
        in_specs=[here] * 2,
        out_specs=here,
        out_shape=jax.ShapeDtypeStruct((ctx_count, 3 * MODES_TILE, LANES), F32),
        compiler_params=small,
        name="pack",
    )(borders, part)
    returned = lax.all_to_all(repacked, "ctx", split_axis=0, concat_axis=0, tiled=True)

    entries = returned.reshape(halves, blocks, 3 * MODES_TILE, LANES)
    results = outputs_call(signals, rates, conv, grad, entries)
    tiles = returned[:, 2 * MODES_TILE :]
    tiles = tiles + lax.ppermute(tiles, "seq", [(i, i ^ 6) for i in range(seq_count)])
    grad_rows = tiles.reshape(halves, blocks, MODES_TILE, LANES).transpose(0, 2, 1, 3)
    return (*[r[None] for r in results], grad_rows.reshape(modes, channels).T)


def solution(mesh):
    split = P("seq", "ctx", None)
    return jax.shard_map(
        on_device,
        mesh=mesh,
        in_specs=(split, split, split, split, P(), P()),
        out_specs=(split, split, split, split, P()),
        check_vma=False,
    )
```

```python
import functools

import jax
import jax.numpy as jnp
from jax import lax
from jax.experimental import pallas as pl
from jax.experimental.pallas import tpu as pltpu
from jax.sharding import PartitionSpec as P

LANES = 128
SUBS = 8
SPARE = 8
MODES_TILE = 8
F32 = jnp.float32
GROUPS = 4
OUTPUT_COLUMNS = 2
STATE_BLOCKS = (4, 4, 4, 4)
AHEAD = 2
UNROLL = 4
PITCH = 17
SMALL_VMEM = 12 * 1024 * 1024
STATES_VMEM = 58 * 1024 * 1024
OUTPUTS_VMEM = 51 * 1024 * 1024


def sub_index():
    return lax.broadcasted_iota(jnp.int32, (SUBS, LANES), 0)


def scale_of(rates):
    bent = jnp.tanh(rates)
    return jnp.sqrt(2.0 * bent / (1.0 + bent))


def rows_of(tile):
    return [jnp.broadcast_to(tile[m : m + 1], (SUBS, LANES)) for m in range(MODES_TILE)]


def states_kernel(
    query_hbm,
    key_hbm,
    value_hbm,
    cot_hbm,
    rates_hbm,
    packed_hbm,
    before_hbm,
    after_hbm,
    query_ref,
    key_ref,
    value_ref,
    cot_ref,
    rates_ref,
    packed_ref,
    before_ref,
    after_ref,
    rates_arrived,
    arrived,
    sent,
    u_ref,
    a_ref,
    lag_ref,
    lag_sum_ref,
    fwd_ref,
    bwd_ref,
    mid_ref,
):
    tokens, width = query_ref.shape
    steps = tokens // SUBS
    modes = rates_ref.shape[0]
    firsts = [sum(STATE_BLOCKS[:n]) for n in range(len(STATE_BLOCKS))]
    pairs = ((query_hbm, query_ref), (key_hbm, key_ref), (value_hbm, value_ref), (cot_hbm, cot_ref))

    def fetches(group):
        lanes = pl.ds(firsts[group] * LANES, STATE_BLOCKS[group] * LANES)
        return [
            pltpu.make_async_copy(source.at[:, lanes], target.at[:, lanes], arrived.at[n, group])
            for n, (source, target) in enumerate(pairs)
        ]

    def stores(group):
        part = pl.ds(firsts[group], STATE_BLOCKS[group])
        rows = pl.ds(0, MODES_TILE * SUBS)
        return [
            pltpu.make_async_copy(packed_ref.at[:, part], packed_hbm.at[:, part], sent.at[0, group]),
            pltpu.make_async_copy(before_ref.at[part, :, rows], before_hbm.at[part], sent.at[1, group]),
            pltpu.make_async_copy(after_ref.at[part, :, rows], after_hbm.at[part], sent.at[2, group]),
        ]

    rates_fetch = pltpu.make_async_copy(rates_hbm, rates_ref, rates_arrived)
    rates_fetch.start()
    for group in range(AHEAD):
        for fetch in fetches(group):
            fetch.start()
    rates_fetch.wait()

    def block(index, carry):
        lanes = pl.ds(pl.multiple_of(index * LANES, LANES), LANES)
        mixed = key_ref[:, lanes].astype(F32) * value_ref[:, lanes].astype(F32)
        adjoint = cot_ref[:, lanes].astype(F32) * query_ref[:, lanes].astype(F32)
        for s in range(SUBS):
            u_ref[s * PITCH : s * PITCH + steps, :] = mixed[s * steps : (s + 1) * steps]
            a_ref[s * PITCH : s * PITCH + steps, :] = adjoint[s * steps : (s + 1) * steps]
        u = [u_ref[pl.ds(i, SUBS, stride=PITCH), :] for i in range(steps)]
        a = [a_ref[pl.ds(i, SUBS, stride=PITCH), :] for i in range(steps)]
        middle = steps // 2
        for lag in range(middle):
            total = None
            for start in (0, middle):
                for i in range(start, start + middle - lag):
                    term = a[lag + i] * u[i]
                    total = term if total is None else total + term
            lag_ref[lag * SUBS : (lag + 1) * SUBS, :] = total
        total = None
        for s in range(SUBS):
            term = lag_ref[pl.ds(s, middle, stride=SUBS), :]
            total = term if total is None else total + term
        lag_sum_ref[...] = total
        for half in range(modes // MODES_TILE):
            rates = rates_ref[half * MODES_TILE : (half + 1) * MODES_TILE, lanes]
            lam_tile = jnp.exp(-rates)
            lam = rows_of(lam_tile)
            fwd = [u_ref[pl.ds(0, SUBS, stride=PITCH), :]] * MODES_TILE
            bwd = [a_ref[pl.ds(steps - 1, SUBS, stride=PITCH), :]] * MODES_TILE
            for i in range(1, steps):
                front = u_ref[pl.ds(i, SUBS, stride=PITCH), :]
                back = a_ref[pl.ds(steps - 1 - i, SUBS, stride=PITCH), :]
                for m in range(MODES_TILE):
                    fwd[m] = lam[m] * fwd[m] + front
                    bwd[m] = lam[m] * bwd[m] + back
                if i == middle - 1:
                    for m in range(MODES_TILE):
                        mid_ref[m * SUBS : (m + 1) * SUBS, :] = fwd[m] * bwd[m]
            for m in range(MODES_TILE):
                fwd_ref[m * SUBS : (m + 1) * SUBS, :] = fwd[m]
                bwd_ref[m * SUBS : (m + 1) * SUBS, :] = bwd[m]
            jump = jnp.exp(rates * -float(steps))
            zero = jnp.zeros((MODES_TILE, LANES), F32)
            before, after, cross, inner = zero, zero, zero, zero
            for s in range(SUBS):
                rows = pl.ds(s, MODES_TILE, stride=SUBS)
                before_ref[index, half, rows, :] = before
                cross = cross + bwd_ref[rows, :] * before + mid_ref[rows, :]
                before = jump * before + fwd_ref[rows, :]
            for s in reversed(range(SUBS)):
                rows = pl.ds(s, MODES_TILE, stride=SUBS)
                after_ref[index, half, rows, :] = after
                after = jump * after + bwd_ref[rows, :]
            for lag in reversed(range(middle)):
                inner = inner * lam_tile + lag_sum_ref[lag : lag + 1, :]
            packed_ref[half, index, 0:MODES_TILE, :] = before
            packed_ref[half, index, MODES_TILE : 2 * MODES_TILE, :] = after
            packed_ref[half, index, 2 * MODES_TILE : 3 * MODES_TILE, :] = inner + lam_tile * cross
        return carry

    for group, (first, count) in enumerate(zip(firsts, STATE_BLOCKS, strict=True)):
        for fetch in fetches(group):
            fetch.wait()
        if group + AHEAD < len(firsts):
            for fetch in fetches(group + AHEAD):
                fetch.start()
        if UNROLL >= count:
            for index in range(first, first + count):
                block(index, 0)
        else:
            lax.fori_loop(first, first + count, block, 0, unroll=UNROLL)
        for store in stores(group):
            store.start()
    for group in range(len(firsts)):
        for store in stores(group):
            store.wait()


def local_kernel(
    query_ref,
    key_ref,
    value_ref,
    cot_ref,
    rates_ref,
    residues_ref,
    before_ref,
    after_ref,
    conv_ref,
    grad_ref,
    u_ref,
    a_ref,
    y_ref,
    g_ref,
):
    tokens, width = query_ref.shape
    steps = tokens // SUBS
    modes = rates_ref.shape[0]

    def block(index, carry):
        lanes = pl.ds(pl.multiple_of(index * LANES, LANES), LANES)
        u_ref[0:tokens] = key_ref[:, lanes].astype(F32) * value_ref[:, lanes].astype(F32)
        a_ref[0:tokens] = cot_ref[:, lanes].astype(F32) * query_ref[:, lanes].astype(F32)
        for half in range(modes // MODES_TILE):
            picked = slice(half * MODES_TILE, (half + 1) * MODES_TILE)
            rates = rates_ref[picked, lanes]
            lam = rows_of(jnp.exp(-rates))
            weight = rows_of(residues_ref[picked, lanes] * scale_of(rates))
            fwd = [before_ref[index, half, m * SUBS : (m + 1) * SUBS, :] for m in range(MODES_TILE)]
            for i in range(steps):
                rows = pl.ds(i, SUBS, stride=steps)
                u = u_ref[rows, :]
                total = y_ref[rows, :] if half else None
                for m in range(MODES_TILE):
                    fwd[m] = lam[m] * fwd[m] + u
                    term = weight[m] * fwd[m]
                    total = term if total is None else total + term
                y_ref[rows, :] = total
            bwd = [after_ref[index, half, m * SUBS : (m + 1) * SUBS, :] for m in range(MODES_TILE)]
            for i in reversed(range(steps)):
                rows = pl.ds(i, SUBS, stride=steps)
                a = a_ref[rows, :]
                total = g_ref[rows, :] if half else None
                for m in range(MODES_TILE):
                    bwd[m] = lam[m] * bwd[m] + a
                    term = weight[m] * bwd[m]
                    total = term if total is None else total + term
                g_ref[rows, :] = total
        conv_ref[:, lanes] = y_ref[0:tokens]
        grad_ref[:, lanes] = g_ref[0:tokens]
        return carry

    lax.fori_loop(0, width // LANES, block, 0)


def scan_kernel(chunk_tokens, per_half, share, states_ref, rates_ref, residues_ref, out_ref, part_ref):
    chunks = states_ref.shape[0]
    rank = lax.axis_index("ctx")
    rows = pl.ds(pl.multiple_of((rank // per_half) * MODES_TILE, MODES_TILE), MODES_TILE)
    lanes = pl.ds(pl.multiple_of((rank % per_half) * LANES, LANES), LANES)
    rates = rates_ref[rows, lanes]
    lam = jnp.exp(-rates)
    jump = jnp.exp(rates * -float(chunk_tokens))
    scaling = scale_of(rates)
    entry = residues_ref[rows, lanes] * scaling * lam
    zero = jnp.zeros((MODES_TILE, LANES), F32)
    fwd, cross, inner = zero, zero, zero
    for j in range(chunks):
        out_ref[j, 0:MODES_TILE] = entry * fwd
        cross = cross + states_ref[j, MODES_TILE : 2 * MODES_TILE] * fwd
        inner = inner + states_ref[j, 2 * MODES_TILE : 3 * MODES_TILE]
        fwd = jump * fwd + states_ref[j, 0:MODES_TILE]
    bwd = zero
    for j in reversed(range(chunks)):
        out_ref[j, MODES_TILE : 2 * MODES_TILE] = entry * bwd
        bwd = jump * bwd + states_ref[j, MODES_TILE : 2 * MODES_TILE]
    part = (inner + lam * cross) * scaling * share
    part_ref[...] = part


def pack_kernel(states_ref, part_ref, out_ref):
    for j in range(out_ref.shape[0]):
        out_ref[j, 0 : 2 * MODES_TILE] = states_ref[j]
        out_ref[j, 2 * MODES_TILE : 3 * MODES_TILE] = part_ref[...]


def output_kernel(
    query_ref,
    key_ref,
    value_ref,
    cot_ref,
    rates_ref,
    conv_hbm,
    grad_hbm,
    entry_ref,
    out_hbm,
    grad_query_hbm,
    grad_key_hbm,
    grad_value_hbm,
    conv_ref,
    grad_ref,
    out_ref,
    grad_query_ref,
    grad_key_ref,
    grad_value_ref,
    arrived,
    sent,
    y_ref,
    g_ref,
):
    tokens, width = query_ref.shape
    modes = rates_ref.shape[0]
    groups = tokens // SUBS
    sub = sub_index().astype(F32)
    columns = sent.shape[1]
    span = width // columns
    pairs = (
        (out_ref, out_hbm),
        (grad_query_ref, grad_query_hbm),
        (grad_key_ref, grad_key_hbm),
        (grad_value_ref, grad_value_hbm),
    )

    inputs = (
        (conv_hbm, conv_ref),
        (grad_hbm, grad_ref),
    )

    def fetches(column):
        lanes = pl.ds(column * span, span)
        return [
            pltpu.make_async_copy(source.at[:, lanes], target.at[:, lanes], arrived.at[n, column])
            for n, (source, target) in enumerate(inputs)
        ]

    for column in range(columns):
        for fetch in fetches(column):
            fetch.start()

    def stores(column):
        lanes = pl.ds(column * span, span)
        return [
            pltpu.make_async_copy(source.at[:, lanes], target.at[:, lanes], sent.at[n, column])
            for n, (source, target) in enumerate(pairs)
        ]

    def entry(index, carry):
        lanes = pl.ds(pl.multiple_of(index * LANES, LANES), LANES)
        rates = [
            rates_ref[half * MODES_TILE : (half + 1) * MODES_TILE, lanes]
            for half in range(modes // MODES_TILE)
        ]
        for part, place, target in ((0, sub, y_ref), (1, SUBS - 1 - sub, g_ref)):
            state, jump = [], []
            for half, rate in enumerate(rates):
                row = rows_of(rate)
                jump += rows_of(jnp.exp(rate * -float(SUBS)))
                start = rows_of(entry_ref[half, index, part * MODES_TILE : (part + 1) * MODES_TILE, :])
                state += [start[m] * jnp.exp(-row[m] * place) for m in range(MODES_TILE)]
            for i in range(groups):
                at = groups - 1 - i if part else i
                total = state[0]
                for term in state[1:]:
                    total = total + term
                target[at * SUBS : (at + 1) * SUBS, lanes] = total
                state = [s * j for s, j in zip(state, jump, strict=True)]
        return carry

    def finish(index, carry):
        lanes = pl.ds(pl.multiple_of(index * LANES, LANES), LANES)
        y = y_ref[:, lanes] + conv_ref[:, lanes]
        g = g_ref[:, lanes] + grad_ref[:, lanes]
        out_ref[:, lanes] = (query_ref[:, lanes].astype(F32) * y).astype(out_ref.dtype)
        grad_query_ref[:, lanes] = (cot_ref[:, lanes].astype(F32) * y).astype(out_ref.dtype)
        grad_key_ref[:, lanes] = (value_ref[:, lanes].astype(F32) * g).astype(out_ref.dtype)
        grad_value_ref[:, lanes] = (key_ref[:, lanes].astype(F32) * g).astype(out_ref.dtype)
        return carry

    count = span // LANES
    for column in range(columns):
        first = column * count
        lax.fori_loop(first, first + count, entry, 0, unroll=True)
        for fetch in fetches(column):
            fetch.wait()
        lax.fori_loop(first, first + count, finish, 0, unroll=True)
        for store in stores(column):
            store.start()
    for column in range(columns):
        for store in stores(column):
            store.wait()


def work(tokens, channels, ops, moved):
    return pl.CostEstimate(
        flops=ops * tokens * channels, bytes_accessed=moved * tokens * channels, transcendentals=0
    )


def states_call(signals, rates):
    tokens, channels = signals[0].shape
    modes = rates.shape[0]
    blocks = channels // LANES
    halves = modes // MODES_TILE
    there = pl.BlockSpec(memory_space=pltpu.HBM)
    border = jax.ShapeDtypeStruct((blocks, halves, MODES_TILE * SUBS, LANES), F32)
    tile = pltpu.VMEM((MODES_TILE * SUBS + SPARE, LANES), F32)
    staged = pltpu.VMEM((blocks, halves, MODES_TILE * SUBS + SPARE, LANES), F32)
    signal_buffer = pltpu.VMEM((tokens, channels), signals[0].dtype)
    return pl.pallas_call(
        states_kernel,
        in_specs=[there] * 5,
        out_specs=[there] * 3,
        out_shape=[jax.ShapeDtypeStruct((halves, blocks, 3 * MODES_TILE, LANES), F32), border, border],
        scratch_shapes=[signal_buffer] * 4
        + [
            pltpu.VMEM((modes, channels), F32),
            pltpu.VMEM((halves, blocks, 3 * MODES_TILE, LANES), F32),
            staged,
            staged,
            pltpu.SemaphoreType.DMA(()),
            pltpu.SemaphoreType.DMA((4, len(STATE_BLOCKS))),
            pltpu.SemaphoreType.DMA((3, len(STATE_BLOCKS))),
            pltpu.VMEM((SUBS * PITCH + 2 * SPARE, LANES), F32),
            pltpu.VMEM((SUBS * PITCH + 2 * SPARE, LANES), F32),
            tile,
            pltpu.VMEM((tokens // SUBS // 2, LANES), F32),
            tile,
            tile,
            tile,
        ],
        compiler_params=pltpu.CompilerParams(vmem_limit_bytes=STATES_VMEM),
        cost_estimate=work(tokens, channels, 96, 16),
        name="states",
    )(*signals, rates)


def outputs_call(signals, rates, conv, grad, entries):
    tokens, channels = signals[0].shape
    signal_type = signals[0].dtype
    signal_buffer = pltpu.VMEM((tokens, channels), signal_type)
    here = pl.BlockSpec(memory_space=pltpu.VMEM)
    there = pl.BlockSpec(memory_space=pltpu.HBM)
    result = jax.ShapeDtypeStruct((tokens, channels), signal_type)
    return pl.pallas_call(
        output_kernel,
        in_specs=[here] * 5 + [there] * 2 + [here],
        out_specs=[there] * 4,
        out_shape=[result] * 4,
        scratch_shapes=[pltpu.VMEM((tokens, channels), F32)] * 2
        + [signal_buffer] * 4
        + [pltpu.SemaphoreType.DMA((2, OUTPUT_COLUMNS)), pltpu.SemaphoreType.DMA((4, OUTPUT_COLUMNS))]
        + [pltpu.VMEM((tokens, channels), F32)] * 2,
        compiler_params=pltpu.CompilerParams(vmem_limit_bytes=OUTPUTS_VMEM),
        cost_estimate=work(tokens, channels, 64, 24),
        name="outputs",
    )(*signals, rates, conv, grad, entries)


def on_device(query_input, key_input, value_input, cotangent, residues, decay_rates):
    tokens, channels = query_input.shape[1:]
    modes = residues.shape[1]
    ctx_count = lax.axis_size("ctx")
    seq_count = lax.axis_size("seq")
    blocks = channels // LANES
    halves = modes // MODES_TILE
    signals = [s[0] for s in (query_input, key_input, value_input, cotangent)]
    rates = decay_rates.T
    modal = residues.T

    here = pl.BlockSpec(memory_space=pltpu.VMEM)
    whole = jax.ShapeDtypeStruct((tokens, channels), F32)
    square = pltpu.VMEM((tokens + 2 * SPARE, LANES), F32)
    small = pltpu.CompilerParams(vmem_limit_bytes=SMALL_VMEM)

    packed, before, after = states_call(signals, rates)

    gathered = lax.all_to_all(
        packed.reshape(ctx_count, 3 * MODES_TILE, LANES), "ctx", split_axis=0, concat_axis=0, tiled=True
    )

    per_step = blocks // GROUPS
    signal_spec = pl.BlockSpec((tokens, per_step * LANES), lambda i: (0, i))
    mode_spec = pl.BlockSpec((modes, per_step * LANES), lambda i: (0, i))
    border_spec = pl.BlockSpec((per_step, halves, MODES_TILE * SUBS, LANES), lambda i: (i, 0, 0, 0))
    conv, grad = pl.pallas_call(
        local_kernel,
        grid=(GROUPS,),
        in_specs=[signal_spec] * 4 + [mode_spec] * 2 + [border_spec] * 2,
        out_specs=[signal_spec] * 2,
        out_shape=[whole] * 2,
        scratch_shapes=[square] * 4,
        cost_estimate=work(tokens, channels, 128, 24),
        name="local",
    )(*signals, rates, modal, before, after)
    gathered, conv, grad = lax.optimization_barrier((gathered, conv, grad))

    borders, part = pl.pallas_call(
        functools.partial(scan_kernel, tokens, blocks, 1.0 / (tokens * ctx_count * seq_count)),
        in_specs=[here] * 3,
        out_specs=[here] * 2,
        out_shape=[
            jax.ShapeDtypeStruct((ctx_count, 2 * MODES_TILE, LANES), F32),
            jax.ShapeDtypeStruct((MODES_TILE, LANES), F32),
        ],
        compiler_params=small,
        name="scan",
    )(gathered, rates, modal)

    near, far, cross = (
        lax.ppermute(part, "seq", [(i, i ^ flip) for i in range(seq_count)]) for flip in (1, 2, 3)
    )
    part = (part + near) + (far + cross)
    repacked = pl.pallas_call(
        pack_kernel,
        in_specs=[here] * 2,
        out_specs=here,
        out_shape=jax.ShapeDtypeStruct((ctx_count, 3 * MODES_TILE, LANES), F32),
        compiler_params=small,
        name="pack",
    )(borders, part)
    returned = lax.all_to_all(repacked, "ctx", split_axis=0, concat_axis=0, tiled=True)

    entries = returned.reshape(halves, blocks, 3 * MODES_TILE, LANES)
    results = outputs_call(signals, rates, conv, grad, entries)
    tiles = returned[:, 2 * MODES_TILE :]
    tiles = tiles + lax.ppermute(tiles, "seq", [(i, i ^ 6) for i in range(seq_count)])
    grad_rows = tiles.reshape(halves, blocks, MODES_TILE, LANES).transpose(0, 2, 1, 3)
    return (*[r[None] for r in results], grad_rows.reshape(modes, channels).T)


def solution(mesh):
    split = P("seq", "ctx", None)
    return jax.shard_map(
        on_device,
        mesh=mesh,
        in_specs=(split, split, split, split, P(), P()),
        out_specs=(split, split, split, split, P()),
        check_vma=False,
    )
```

```python
import functools

import jax
import jax.numpy as jnp
from jax import lax
from jax.experimental import pallas as pl
from jax.experimental.pallas import tpu as pltpu
from jax.sharding import PartitionSpec as P

LANES = 128
SUBS = 8
SPARE = 8
MODES_TILE = 8
F32 = jnp.float32
LOCAL_STEPS = 2
OUTPUT_COLUMNS = 2
STATE_BLOCKS = (4, 4, 4, 4)
AHEAD = 2
UNROLL = 4
PITCH = 17
SMALL_VMEM = 12 * 1024 * 1024
STATES_VMEM = 58 * 1024 * 1024
OUTPUTS_VMEM = 51 * 1024 * 1024


def sub_index():
    return lax.broadcasted_iota(jnp.int32, (SUBS, LANES), 0)


def scale_of(rates):
    bent = jnp.tanh(rates)
    return jnp.sqrt(2.0 * bent / (1.0 + bent))


def rows_of(tile):
    return [jnp.broadcast_to(tile[m : m + 1], (SUBS, LANES)) for m in range(MODES_TILE)]


def states_kernel(
    query_hbm,
    key_hbm,
    value_hbm,
    cot_hbm,
    rates_hbm,
    packed_hbm,
    before_hbm,
    after_hbm,
    query_ref,
    key_ref,
    value_ref,
    cot_ref,
    rates_ref,
    packed_ref,
    before_ref,
    after_ref,
    rates_arrived,
    arrived,
    sent,
    u_ref,
    a_ref,
    lag_ref,
    lag_sum_ref,
    fwd_ref,
    bwd_ref,
    mid_ref,
):
    tokens, width = query_ref.shape
    steps = tokens // SUBS
    modes = rates_ref.shape[0]
    firsts = [sum(STATE_BLOCKS[:n]) for n in range(len(STATE_BLOCKS))]
    pairs = ((query_hbm, query_ref), (key_hbm, key_ref), (value_hbm, value_ref), (cot_hbm, cot_ref))

    def fetches(group):
        lanes = pl.ds(firsts[group] * LANES, STATE_BLOCKS[group] * LANES)
        return [
            pltpu.make_async_copy(source.at[:, lanes], target.at[:, lanes], arrived.at[n, group])
            for n, (source, target) in enumerate(pairs)
        ]

    def stores(group):
        part = pl.ds(firsts[group], STATE_BLOCKS[group])
        rows = pl.ds(0, MODES_TILE * SUBS)
        return [
            pltpu.make_async_copy(packed_ref.at[:, part], packed_hbm.at[:, part], sent.at[0, group]),
            pltpu.make_async_copy(before_ref.at[part, :, rows], before_hbm.at[part], sent.at[1, group]),
            pltpu.make_async_copy(after_ref.at[part, :, rows], after_hbm.at[part], sent.at[2, group]),
        ]

    rates_fetch = pltpu.make_async_copy(rates_hbm, rates_ref, rates_arrived)
    rates_fetch.start()
    for group in range(AHEAD):
        for fetch in fetches(group):
            fetch.start()
    rates_fetch.wait()

    def block(index, carry):
        lanes = pl.ds(pl.multiple_of(index * LANES, LANES), LANES)
        mixed = key_ref[:, lanes].astype(F32) * value_ref[:, lanes].astype(F32)
        adjoint = cot_ref[:, lanes].astype(F32) * query_ref[:, lanes].astype(F32)
        for s in range(SUBS):
            u_ref[s * PITCH : s * PITCH + steps, :] = mixed[s * steps : (s + 1) * steps]
            a_ref[s * PITCH : s * PITCH + steps, :] = adjoint[s * steps : (s + 1) * steps]
        u = [u_ref[pl.ds(i, SUBS, stride=PITCH), :] for i in range(steps)]
        a = [a_ref[pl.ds(i, SUBS, stride=PITCH), :] for i in range(steps)]
        middle = steps // 2
        for lag in range(middle):
            total = None
            for start in (0, middle):
                for i in range(start, start + middle - lag):
                    term = a[lag + i] * u[i]
                    total = term if total is None else total + term
            lag_ref[lag * SUBS : (lag + 1) * SUBS, :] = total
        total = None
        for s in range(SUBS):
            term = lag_ref[pl.ds(s, middle, stride=SUBS), :]
            total = term if total is None else total + term
        lag_sum_ref[...] = total
        for half in range(modes // MODES_TILE):
            rates = rates_ref[half * MODES_TILE : (half + 1) * MODES_TILE, lanes]
            lam_tile = jnp.exp(-rates)
            lam = rows_of(lam_tile)
            fwd = [u_ref[pl.ds(0, SUBS, stride=PITCH), :]] * MODES_TILE
            bwd = [a_ref[pl.ds(steps - 1, SUBS, stride=PITCH), :]] * MODES_TILE
            for i in range(1, steps):
                front = u_ref[pl.ds(i, SUBS, stride=PITCH), :]
                back = a_ref[pl.ds(steps - 1 - i, SUBS, stride=PITCH), :]
                for m in range(MODES_TILE):
                    fwd[m] = lam[m] * fwd[m] + front
                    bwd[m] = lam[m] * bwd[m] + back
                if i == middle - 1:
                    for m in range(MODES_TILE):
                        mid_ref[m * SUBS : (m + 1) * SUBS, :] = fwd[m] * bwd[m]
            for m in range(MODES_TILE):
                fwd_ref[m * SUBS : (m + 1) * SUBS, :] = fwd[m]
                bwd_ref[m * SUBS : (m + 1) * SUBS, :] = bwd[m]
            jump = jnp.exp(rates * -float(steps))
            zero = jnp.zeros((MODES_TILE, LANES), F32)
            before, after, cross, inner = zero, zero, zero, zero
            for s in range(SUBS):
                rows = pl.ds(s, MODES_TILE, stride=SUBS)
                before_ref[index, half, rows, :] = before
                cross = cross + bwd_ref[rows, :] * before + mid_ref[rows, :]
                before = jump * before + fwd_ref[rows, :]
            for s in reversed(range(SUBS)):
                rows = pl.ds(s, MODES_TILE, stride=SUBS)
                after_ref[index, half, rows, :] = after
                after = jump * after + bwd_ref[rows, :]
            for lag in reversed(range(middle)):
                inner = inner * lam_tile + lag_sum_ref[lag : lag + 1, :]
            packed_ref[half, index, 0:MODES_TILE, :] = before
            packed_ref[half, index, MODES_TILE : 2 * MODES_TILE, :] = after
            packed_ref[half, index, 2 * MODES_TILE : 3 * MODES_TILE, :] = inner + lam_tile * cross
        return carry

    for group, (first, count) in enumerate(zip(firsts, STATE_BLOCKS, strict=True)):
        for fetch in fetches(group):
            fetch.wait()
        if group + AHEAD < len(firsts):
            for fetch in fetches(group + AHEAD):
                fetch.start()
        if UNROLL >= count:
            for index in range(first, first + count):
                block(index, 0)
        else:
            lax.fori_loop(first, first + count, block, 0, unroll=UNROLL)
        for store in stores(group):
            store.start()
    for group in range(len(firsts)):
        for store in stores(group):
            store.wait()


def local_kernel(
    query_ref,
    key_ref,
    value_ref,
    cot_ref,
    rates_ref,
    residues_ref,
    before_ref,
    after_ref,
    conv_ref,
    grad_ref,
    u_ref,
    a_ref,
    y_ref,
    g_ref,
):
    tokens, width = query_ref.shape
    steps = tokens // SUBS
    modes = rates_ref.shape[0]

    def block(index, carry):
        lanes = pl.ds(pl.multiple_of(index * LANES, LANES), LANES)
        u_ref[0:tokens] = key_ref[:, lanes].astype(F32) * value_ref[:, lanes].astype(F32)
        a_ref[0:tokens] = cot_ref[:, lanes].astype(F32) * query_ref[:, lanes].astype(F32)
        for half in range(modes // MODES_TILE):
            picked = slice(half * MODES_TILE, (half + 1) * MODES_TILE)
            rates = rates_ref[picked, lanes]
            lam = rows_of(jnp.exp(-rates))
            weight = rows_of(residues_ref[picked, lanes] * scale_of(rates))
            fwd = [before_ref[index, half, m * SUBS : (m + 1) * SUBS, :] for m in range(MODES_TILE)]
            for i in range(steps):
                rows = pl.ds(i, SUBS, stride=steps)
                u = u_ref[rows, :]
                total = y_ref[rows, :] if half else None
                for m in range(MODES_TILE):
                    fwd[m] = lam[m] * fwd[m] + u
                    term = weight[m] * fwd[m]
                    total = term if total is None else total + term
                y_ref[rows, :] = total
            bwd = [after_ref[index, half, m * SUBS : (m + 1) * SUBS, :] for m in range(MODES_TILE)]
            for i in reversed(range(steps)):
                rows = pl.ds(i, SUBS, stride=steps)
                a = a_ref[rows, :]
                total = g_ref[rows, :] if half else None
                for m in range(MODES_TILE):
                    bwd[m] = lam[m] * bwd[m] + a
                    term = weight[m] * bwd[m]
                    total = term if total is None else total + term
                g_ref[rows, :] = total
        conv_ref[:, lanes] = y_ref[0:tokens]
        grad_ref[:, lanes] = g_ref[0:tokens]
        return carry

    lax.fori_loop(0, width // LANES, block, 0)


def scan_kernel(chunk_tokens, per_half, share, states_ref, rates_ref, residues_ref, out_ref, part_ref):
    chunks = states_ref.shape[0]
    rank = lax.axis_index("ctx")
    rows = pl.ds(pl.multiple_of((rank // per_half) * MODES_TILE, MODES_TILE), MODES_TILE)
    lanes = pl.ds(pl.multiple_of((rank % per_half) * LANES, LANES), LANES)
    rates = rates_ref[rows, lanes]
    lam = jnp.exp(-rates)
    jump = jnp.exp(rates * -float(chunk_tokens))
    scaling = scale_of(rates)
    entry = residues_ref[rows, lanes] * scaling * lam
    zero = jnp.zeros((MODES_TILE, LANES), F32)
    fwd, cross, inner = zero, zero, zero
    for j in range(chunks):
        out_ref[j, 0:MODES_TILE] = entry * fwd
        cross = cross + states_ref[j, MODES_TILE : 2 * MODES_TILE] * fwd
        inner = inner + states_ref[j, 2 * MODES_TILE : 3 * MODES_TILE]
        fwd = jump * fwd + states_ref[j, 0:MODES_TILE]
    bwd = zero
    for j in reversed(range(chunks)):
        out_ref[j, MODES_TILE : 2 * MODES_TILE] = entry * bwd
        bwd = jump * bwd + states_ref[j, MODES_TILE : 2 * MODES_TILE]
    part = (inner + lam * cross) * scaling * share
    part_ref[...] = part


def pack_kernel(states_ref, part_ref, out_ref):
    for j in range(out_ref.shape[0]):
        out_ref[j, 0 : 2 * MODES_TILE] = states_ref[j]
        out_ref[j, 2 * MODES_TILE : 3 * MODES_TILE] = part_ref[...]


def output_kernel(
    query_ref,
    key_ref,
    value_ref,
    cot_ref,
    rates_ref,
    conv_hbm,
    grad_hbm,
    entry_ref,
    out_hbm,
    grad_query_hbm,
    grad_key_hbm,
    grad_value_hbm,
    conv_ref,
    grad_ref,
    out_ref,
    grad_query_ref,
    grad_key_ref,
    grad_value_ref,
    arrived,
    sent,
    y_ref,
    g_ref,
):
    tokens, width = query_ref.shape
    modes = rates_ref.shape[0]
    groups = tokens // SUBS
    sub = sub_index().astype(F32)
    columns = sent.shape[1]
    span = width // columns
    pairs = (
        (out_ref, out_hbm),
        (grad_query_ref, grad_query_hbm),
        (grad_key_ref, grad_key_hbm),
        (grad_value_ref, grad_value_hbm),
    )

    inputs = (
        (conv_hbm, conv_ref),
        (grad_hbm, grad_ref),
    )

    def fetches(column):
        lanes = pl.ds(column * span, span)
        return [
            pltpu.make_async_copy(source.at[:, lanes], target.at[:, lanes], arrived.at[n, column])
            for n, (source, target) in enumerate(inputs)
        ]

    for column in range(columns):
        for fetch in fetches(column):
            fetch.start()

    def stores(column):
        lanes = pl.ds(column * span, span)
        return [
            pltpu.make_async_copy(source.at[:, lanes], target.at[:, lanes], sent.at[n, column])
            for n, (source, target) in enumerate(pairs)
        ]

    def entry(index, carry):
        lanes = pl.ds(pl.multiple_of(index * LANES, LANES), LANES)
        for half in range(modes // MODES_TILE):
            picked = slice(half * MODES_TILE, (half + 1) * MODES_TILE)
            rates = rates_ref[picked, lanes]
            row = rows_of(rates)
            jump = rows_of(jnp.exp(rates * -float(SUBS)))
            early = rows_of(entry_ref[half, index, 0:MODES_TILE, :])
            late = rows_of(entry_ref[half, index, MODES_TILE : 2 * MODES_TILE, :])
            fwd = [early[m] * jnp.exp(-row[m] * sub) for m in range(MODES_TILE)]
            bwd = [late[m] * jnp.exp(-row[m] * (SUBS - 1 - sub)) for m in range(MODES_TILE)]
            for i in range(groups):
                rows = slice(i * SUBS, (i + 1) * SUBS)
                total = y_ref[rows, lanes] if half else None
                for m in range(MODES_TILE):
                    total = fwd[m] if total is None else total + fwd[m]
                    fwd[m] = fwd[m] * jump[m]
                y_ref[rows, lanes] = total
                rows = slice((groups - 1 - i) * SUBS, (groups - i) * SUBS)
                total = g_ref[rows, lanes] if half else None
                for m in range(MODES_TILE):
                    total = bwd[m] if total is None else total + bwd[m]
                    bwd[m] = bwd[m] * jump[m]
                g_ref[rows, lanes] = total
        return carry

    def finish(index, carry):
        lanes = pl.ds(pl.multiple_of(index * LANES, LANES), LANES)
        y = y_ref[:, lanes] + conv_ref[:, lanes]
        g = g_ref[:, lanes] + grad_ref[:, lanes]
        out_ref[:, lanes] = (query_ref[:, lanes].astype(F32) * y).astype(out_ref.dtype)
        grad_query_ref[:, lanes] = (cot_ref[:, lanes].astype(F32) * y).astype(out_ref.dtype)
        grad_key_ref[:, lanes] = (value_ref[:, lanes].astype(F32) * g).astype(out_ref.dtype)
        grad_value_ref[:, lanes] = (key_ref[:, lanes].astype(F32) * g).astype(out_ref.dtype)
        return carry

    count = span // LANES
    for column in range(columns):
        first = column * count
        lax.fori_loop(first, first + count, entry, 0, unroll=True)
        for fetch in fetches(column):
            fetch.wait()
        lax.fori_loop(first, first + count, finish, 0, unroll=True)
        for store in stores(column):
            store.start()
    for column in range(columns):
        for store in stores(column):
            store.wait()


def work(tokens, channels, ops, moved):
    return pl.CostEstimate(
        flops=ops * tokens * channels, bytes_accessed=moved * tokens * channels, transcendentals=0
    )


def states_call(signals, rates):
    tokens, channels = signals[0].shape
    modes = rates.shape[0]
    blocks = channels // LANES
    halves = modes // MODES_TILE
    there = pl.BlockSpec(memory_space=pltpu.HBM)
    border = jax.ShapeDtypeStruct((blocks, halves, MODES_TILE * SUBS, LANES), F32)
    tile = pltpu.VMEM((MODES_TILE * SUBS + SPARE, LANES), F32)
    staged = pltpu.VMEM((blocks, halves, MODES_TILE * SUBS + SPARE, LANES), F32)
    signal_buffer = pltpu.VMEM((tokens, channels), signals[0].dtype)
    return pl.pallas_call(
        states_kernel,
        in_specs=[there] * 5,
        out_specs=[there] * 3,
        out_shape=[jax.ShapeDtypeStruct((halves, blocks, 3 * MODES_TILE, LANES), F32), border, border],
        scratch_shapes=[signal_buffer] * 4
        + [
            pltpu.VMEM((modes, channels), F32),
            pltpu.VMEM((halves, blocks, 3 * MODES_TILE, LANES), F32),
            staged,
            staged,
            pltpu.SemaphoreType.DMA(()),
            pltpu.SemaphoreType.DMA((4, len(STATE_BLOCKS))),
            pltpu.SemaphoreType.DMA((3, len(STATE_BLOCKS))),
            pltpu.VMEM((SUBS * PITCH + 2 * SPARE, LANES), F32),
            pltpu.VMEM((SUBS * PITCH + 2 * SPARE, LANES), F32),
            tile,
            pltpu.VMEM((tokens // SUBS // 2, LANES), F32),
            tile,
            tile,
            tile,
        ],
        compiler_params=pltpu.CompilerParams(vmem_limit_bytes=STATES_VMEM),
        cost_estimate=work(tokens, channels, 96, 16),
        name="states",
    )(*signals, rates)


def outputs_call(signals, rates, conv, grad, entries):
    tokens, channels = signals[0].shape
    signal_type = signals[0].dtype
    signal_buffer = pltpu.VMEM((tokens, channels), signal_type)
    here = pl.BlockSpec(memory_space=pltpu.VMEM)
    there = pl.BlockSpec(memory_space=pltpu.HBM)
    result = jax.ShapeDtypeStruct((tokens, channels), signal_type)
    return pl.pallas_call(
        output_kernel,
        in_specs=[here] * 5 + [there] * 2 + [here],
        out_specs=[there] * 4,
        out_shape=[result] * 4,
        scratch_shapes=[pltpu.VMEM((tokens, channels), F32)] * 2
        + [signal_buffer] * 4
        + [pltpu.SemaphoreType.DMA((2, OUTPUT_COLUMNS)), pltpu.SemaphoreType.DMA((4, OUTPUT_COLUMNS))]
        + [pltpu.VMEM((tokens, channels), F32)] * 2,
        compiler_params=pltpu.CompilerParams(vmem_limit_bytes=OUTPUTS_VMEM),
        cost_estimate=work(tokens, channels, 64, 24),
        name="outputs",
    )(*signals, rates, conv, grad, entries)


def on_device(query_input, key_input, value_input, cotangent, residues, decay_rates):
    tokens, channels = query_input.shape[1:]
    modes = residues.shape[1]
    ctx_count = lax.axis_size("ctx")
    seq_count = lax.axis_size("seq")
    blocks = channels // LANES
    halves = modes // MODES_TILE
    signals = [s[0] for s in (query_input, key_input, value_input, cotangent)]
    rates = decay_rates.T
    modal = residues.T

    here = pl.BlockSpec(memory_space=pltpu.VMEM)
    whole = jax.ShapeDtypeStruct((tokens, channels), F32)
    square = pltpu.VMEM((tokens + 2 * SPARE, LANES), F32)
    small = pltpu.CompilerParams(vmem_limit_bytes=SMALL_VMEM)

    packed, before, after = states_call(signals, rates)

    gathered = lax.all_to_all(
        packed.reshape(ctx_count, 3 * MODES_TILE, LANES), "ctx", split_axis=0, concat_axis=0, tiled=True
    )

    per_step = blocks // LOCAL_STEPS
    signal_spec = pl.BlockSpec((tokens, per_step * LANES), lambda i: (0, i))
    mode_spec = pl.BlockSpec((modes, per_step * LANES), lambda i: (0, i))
    border_spec = pl.BlockSpec((per_step, halves, MODES_TILE * SUBS, LANES), lambda i: (i, 0, 0, 0))
    conv, grad = pl.pallas_call(
        local_kernel,
        grid=(LOCAL_STEPS,),
        in_specs=[signal_spec] * 4 + [mode_spec] * 2 + [border_spec] * 2,
        out_specs=[signal_spec] * 2,
        out_shape=[whole] * 2,
        scratch_shapes=[square] * 4,
        cost_estimate=work(tokens, channels, 128, 24),
        name="local",
    )(*signals, rates, modal, before, after)
    gathered, conv, grad = lax.optimization_barrier((gathered, conv, grad))

    borders, part = pl.pallas_call(
        functools.partial(scan_kernel, tokens, blocks, 1.0 / (tokens * ctx_count * seq_count)),
        in_specs=[here] * 3,
        out_specs=[here] * 2,
        out_shape=[
            jax.ShapeDtypeStruct((ctx_count, 2 * MODES_TILE, LANES), F32),
            jax.ShapeDtypeStruct((MODES_TILE, LANES), F32),
        ],
        compiler_params=small,
        name="scan",
    )(gathered, rates, modal)

    near, far, cross = (
        lax.ppermute(part, "seq", [(i, i ^ flip) for i in range(seq_count)]) for flip in (1, 2, 3)
    )
    part = (part + near) + (far + cross)
    repacked = pl.pallas_call(
        pack_kernel,
        in_specs=[here] * 2,
        out_specs=here,
        out_shape=jax.ShapeDtypeStruct((ctx_count, 3 * MODES_TILE, LANES), F32),
        compiler_params=small,
        name="pack",
    )(borders, part)
    returned = lax.all_to_all(repacked, "ctx", split_axis=0, concat_axis=0, tiled=True)

    entries = returned.reshape(halves, blocks, 3 * MODES_TILE, LANES)
    results = outputs_call(signals, rates, conv, grad, entries)
    tiles = returned[:, 2 * MODES_TILE :]
    tiles = tiles + lax.ppermute(tiles, "seq", [(i, i ^ 6) for i in range(seq_count)])
    grad_rows = tiles.reshape(halves, blocks, MODES_TILE, LANES).transpose(0, 2, 1, 3)
    return (*[r[None] for r in results], grad_rows.reshape(modes, channels).T)


def solution(mesh):
    split = P("seq", "ctx", None)
    return jax.shard_map(
        on_device,
        mesh=mesh,
        in_specs=(split, split, split, split, P(), P()),
        out_specs=(split, split, split, split, P()),
        check_vma=False,
    )
```
